512 devices in a mesh: elec: 64 (over x, y, core), therm: 8 (over z).
Axes of the slice: x: 4, y: 8, z: 8, core: 2. Of those that a mesh axis runs over, the one named last changes fastest.
Arguments:
- injected_amperage: bfloat16 [16384, 64, 128], P(('elec', 'therm')), may hold values from -6 to 6
- voltage_self_admittance: float32 [16384, 64], P(('elec', 'therm')), may hold values from 1.2 to 2.5
- voltage_coupling_tiles: bfloat16 [16384, 4, 64, 64], P(('elec', 'therm')), may hold values from -0.5 to 0.5
- voltage_partner_tile_ids: int32 [16384, 4], P(('elec', 'therm')), may hold values from 0 to 31
- interface_tiles_per_level: int32 [2048, 2], P(('elec', 'therm')), may hold values from 0 to 31
- interface_admittance: bfloat16 [4096, 64, 64], P(('elec', 'therm')), may hold values from -0.5 to 0.5
- warmth_receiver_layer: int32 [16384, 1], P(('elec', 'therm')), may hold values from 0 to 7; in each aligned block of 32 rows (0 to 31, 32 to 63, ...) at most 8 rows name the same one
- warmth_receiver_tile: int32 [16384], P(('elec', 'therm')), may hold values from 0 to 31
- warmth_values: bfloat16 [16384, 64, 128], P(('elec', 'therm')), may hold values from -4 to 4
- warmth_self_coefficient: float32 [16384, 64], P(('elec', 'therm')), may hold values from 1 to 3
- warmth_coupling_tiles: bfloat16 [16384, 3, 64, 64], P(('elec', 'therm')), may hold values from -0.4375 to 0.4375
- warmth_partner_tile_ids: int32 [16384, 3], P(('elec', 'therm')), may hold values from 0 to 31
- layer_boundary_couplings: bfloat16 [2048, 64, 64], P(('elec', 'therm')), may hold values from -0.4375 to 0.4375
- substance_kind: int32 [16384, 64], P(('elec', 'therm')), may hold values from 0 to 7
- reference_material_kappas: float32 [8], replicated, may hold values from 0.5 to 4
- warmth_storage_per_point: float32 [16384, 64], P(('elec', 'therm')), may hold values from 1 to 4
Outputs:
- voltage_solution: bfloat16 [16384, 64, 128], P(('elec', 'therm'))
- advanced_warmth_values: float32 [16384, 64, 128], P(('elec', 'therm'))
The draws below stay inside these ranges and needn't reach their ends.
Inputs may be any that keep to these rules, and one draw needn't show every extreme that they name: `warmth_receiver_layer`: among the 32 blocks of one device at most 8 name the same owner, and exactly 8 do for some owner. `voltage_partner_tile_ids`: indexes a block of the same device. `interface_tiles_per_level`: indexes a block of the same device. `warmth_receiver_tile`: indexes a thermal block of the owner. `warmth_partner_tile_ids`: indexes a thermal block of the same device.
All inputs are finite; a program needn't handle non-finite values.
Results may differ from the reference program's by a relative error of at most 0.025.
Values may be sent and summed in bfloat16 or wider, within the bound.
A program may use at most 64 MiB of HBM per device.

```python
import math
import jax
import jax.numpy as jnp
import numpy as np
from jax import lax

TILE_POINT_COUNT = 64
LOAD_REGIMES = 128
EB_DEV = 32
K_LOC = 4
K_T = 3
LEVELS = 4
FACE = 2
SWEEPS = 5
ZB = 2
MATS = 8
UNIT_WARMTH_TILES = 32
VOLTAGE_TILES = 16384
WARMTH_TILES = 16384
CAP = 8
N_ELEC = 64
N_THERM = 8


def plant(result, stream_key, smallest, largest):
    spot = [jax.random.randint(jax.random.fold_in(stream_key, axis), (), 0, length) for axis, length in enumerate(result.shape)]
    widest = result.shape.index(max(result.shape))
    next_to = spot[:widest] + [(spot[widest] + 1) % result.shape[widest]] + spot[widest + 1:]
    return result.at[tuple(spot)].set(smallest).at[tuple(next_to)].set(largest)


def block_levels(stream_key, shape, split, least, top_value):
    def one(position, parts):
        steps = jax.random.uniform(jax.random.fold_in(jax.random.fold_in(stream_key, 6), position), (parts,), jnp.float32, least / len(split), top_value / len(split))
        return jnp.repeat(jnp.exp(steps), shape[position] // parts).reshape((-1,) + (1,) * (len(shape) - position - 1))

    level = one(*split[0])
    for cut in split[1:]:
        level = level * one(*cut)
    return level


def routed_block(stream_key, own, number, rows, amount, top, reach, slope):
    order = jax.random.permutation(stream_key, amount)
    packed, usual = portions_of(amount, rows * top, reach, slope, True), portions_of(amount, rows * top, reach, slope, False)
    places = jnp.arange(amount)

    def named(sizes, rotation):
        used = int((sizes > 0).sum())
        fixed = max(1, used // 4)
        moved = fixed + (places - fixed + rotation * (used - fixed)) % max(1, amount - fixed)
        return jnp.zeros((amount,), jnp.int32).at[order[jnp.where(places < fixed, places, moved)]].set(jnp.asarray(sizes, jnp.int32))

    sizes = jnp.where(number % 4 == 0, named(packed, number // 4), named(usual, number - number // 4 - 1))
    mixed = jax.random.permutation(jax.random.fold_in(own, 3), amount)
    donor, taker = mixed[0:amount // 2 * 2:2], mixed[1:amount // 2 * 2:2]
    room = jnp.minimum(sizes[donor] - 1, reach - sizes[taker]) // 2
    room = jnp.where((donor == order[0]) | (taker == order[0]) | (sizes[taker] == 0), 0, jnp.maximum(room, 0))
    moved = jax.random.randint(jax.random.fold_in(own, 4), (amount // 2,), 0, 1 << 20) % (room + 1)
    sizes = sizes.at[donor].add(-moved).at[taker].add(moved)
    labels = jnp.searchsorted(jnp.cumsum(sizes), jnp.arange(rows * top), side="right").astype(jnp.int32)
    table = labels.reshape(top, rows).T
    table = table[jax.random.permutation(jax.random.fold_in(own, 1), rows)]
    rotation = jax.random.randint(jax.random.fold_in(own, 2), (rows, 1), 0, top)
    return jnp.take_along_axis(table, (jnp.arange(top)[None, :] + rotation) % top, axis=1)


def portions_of(amount, total, most, slope, full):
    loads = [(1 << 20) // math.isqrt(standing ** slope) + 1 for standing in range(1, amount + 1)]
    largest = most if full else min(most, max(-(-total // amount), total * loads[0] // sum(loads)))
    least = 1 if total - largest >= amount - 1 else 0
    given, spare = [largest] + [least] * (amount - 1), total - largest - least * (amount - 1)
    while spare > 0:
        candidates = [i for i in range(1, amount) if given[i] < largest] or [i for i in range(1, amount) if given[i] < most]
        whole, budget = sum([loads[i] for i in candidates]), spare
        for i in candidates:
            addition = min(most - given[i], max(1, budget * loads[i] // whole), spare)
            given[i] = given[i] + addition
            spare = spare - addition
    return np.array(given)


def scatter_about(own_key, extent, deviation, limit, split=(), dtype=jnp.bfloat16):
    values = deviation * jax.random.normal(own_key, extent, jnp.float32)
    if split:
        values = values * block_levels(own_key, extent, split, -0.22, 0.18)
    return jnp.clip(values, -limit, limit).astype(dtype)


def setup_inputs(seed: int = 0) -> dict:
    arg_keys = jax.random.split(jax.random.key(seed), 17)
    injected_amperage = scatter_about(arg_keys[0], (VOLTAGE_TILES, TILE_POINT_COUNT, LOAD_REGIMES), 1.0, 6.0, ((0, 512),))
    voltage_self_admittance = jnp.clip(jnp.exp(math.log(2.5) - 0.73396914 * jax.random.uniform(arg_keys[1], (VOLTAGE_TILES, TILE_POINT_COUNT), jnp.float32) ** block_levels(arg_keys[1], (VOLTAGE_TILES, TILE_POINT_COUNT), ((0, 512),), -0.2, 0.2)), 1.2, 2.5)
    voltage_coupling_tiles = scatter_about(arg_keys[2], (VOLTAGE_TILES, K_LOC, TILE_POINT_COUNT, TILE_POINT_COUNT), (TILE_POINT_COUNT * K_LOC * 16 // 25) ** -0.5, 0.5, ((0, 512),))
    voltage_partner_tile_ids = plant(jax.random.randint(arg_keys[3], (VOLTAGE_TILES, K_LOC), 0, EB_DEV), jax.random.fold_in(arg_keys[3], 1), 0, EB_DEV - 1).astype(jnp.int32)
    interface_tiles_per_level = plant(jax.random.randint(arg_keys[4], (N_ELEC * N_THERM * LEVELS, FACE), 0, EB_DEV), jax.random.fold_in(arg_keys[4], 1), 0, EB_DEV - 1).astype(jnp.int32)
    interface_admittance = scatter_about(arg_keys[5], (N_ELEC * N_THERM * LEVELS * FACE, TILE_POINT_COUNT, TILE_POINT_COUNT), (TILE_POINT_COUNT * K_LOC * 16 // 25) ** -0.5, 0.5, ((0, 512),))
    warmth_receiver_layer_keys = jax.random.split(jax.random.fold_in(arg_keys[6], 1), VOLTAGE_TILES // EB_DEV)
    warmth_receiver_layer_turns = jax.random.permutation(jax.random.fold_in(arg_keys[6], 3), VOLTAGE_TILES // EB_DEV)
    warmth_receiver_layer = jax.vmap(lambda own, number: routed_block(jax.random.fold_in(arg_keys[6], 2), own, number, EB_DEV, N_THERM, 1, CAP, 2))(warmth_receiver_layer_keys, warmth_receiver_layer_turns).reshape((VOLTAGE_TILES, 1))
    warmth_receiver_tile = plant(jax.random.randint(arg_keys[7], (VOLTAGE_TILES,), 0, UNIT_WARMTH_TILES), jax.random.fold_in(arg_keys[7], 1), 0, UNIT_WARMTH_TILES - 1).astype(jnp.int32)
    warmth_values = scatter_about(arg_keys[8], (WARMTH_TILES, TILE_POINT_COUNT, LOAD_REGIMES), 1.0, 4.0, ((0, 512),))
    warmth_self_coefficient = jnp.clip(jnp.exp(math.log(3.0) - 1.0986123 * jax.random.uniform(arg_keys[9], (WARMTH_TILES, TILE_POINT_COUNT), jnp.float32) ** block_levels(arg_keys[9], (WARMTH_TILES, TILE_POINT_COUNT), ((0, 512),), -0.2, 0.2)), 1.0, 3.0)
    warmth_coupling_tiles = scatter_about(arg_keys[10], (WARMTH_TILES, K_T, TILE_POINT_COUNT, TILE_POINT_COUNT), (TILE_POINT_COUNT * K_T) ** -0.5, 0.4375, ((0, 512),))
    warmth_partner_tile_ids = plant(jax.random.randint(arg_keys[11], (WARMTH_TILES, K_T), 0, UNIT_WARMTH_TILES), jax.random.fold_in(arg_keys[11], 1), 0, UNIT_WARMTH_TILES - 1).astype(jnp.int32)
    layer_boundary_couplings = scatter_about(arg_keys[12], (N_ELEC * N_THERM * 2 * ZB, TILE_POINT_COUNT, TILE_POINT_COUNT), (TILE_POINT_COUNT * K_T) ** -0.5, 0.4375, ((0, 512),))
    substance_kind = plant(jax.random.randint(arg_keys[13], (WARMTH_TILES, TILE_POINT_COUNT), 0, MATS), jax.random.fold_in(arg_keys[13], 1), 0, MATS - 1).astype(jnp.int32)
    reference_material_kappas = jnp.clip(jnp.exp(jax.random.uniform(arg_keys[14], (MATS,), jnp.float32, math.log(0.5), math.log(4.0))), 0.5, 4.0)
    warmth_storage_per_point = jnp.clip(jnp.exp(math.log(4.0) - 1.3862944 * jax.random.uniform(arg_keys[15], (WARMTH_TILES, TILE_POINT_COUNT), jnp.float32) ** block_levels(arg_keys[15], (WARMTH_TILES, TILE_POINT_COUNT), ((0, 512),), -0.2, 0.2)), 1.0, 4.0)
    return dict(injected_amperage=injected_amperage, voltage_self_admittance=voltage_self_admittance, voltage_coupling_tiles=voltage_coupling_tiles, voltage_partner_tile_ids=voltage_partner_tile_ids, interface_tiles_per_level=interface_tiles_per_level, interface_admittance=interface_admittance, warmth_receiver_layer=warmth_receiver_layer, warmth_receiver_tile=warmth_receiver_tile, warmth_values=warmth_values, warmth_self_coefficient=warmth_self_coefficient, warmth_coupling_tiles=warmth_coupling_tiles, warmth_partner_tile_ids=warmth_partner_tile_ids, layer_boundary_couplings=layer_boundary_couplings, substance_kind=substance_kind, reference_material_kappas=reference_material_kappas, warmth_storage_per_point=warmth_storage_per_point)


relax_factor = 0.8
time_increment = 0.5


def near_product(operands):
    field_b, near_blocks, near_index = operands
    picked = field_b[near_index]
    return jnp.einsum("rkab,rkbc->rac", near_blocks.astype(jnp.float32), picked.astype(jnp.float32))


def take_rows(field_b, index_rows):
    return field_b[index_rows]


def add_rows(total, index_rows, terms):
    return total.at[index_rows].add(terms)


def electric_apply(field_b, voltage_self_admittance, voltage_coupling_tiles, voltage_partner_tile_ids, interface_tiles_per_level, interface_admittance):
    unit_count_overall = N_ELEC * N_THERM
    near_terms = lax.map(near_product, (field_b, voltage_coupling_tiles, voltage_partner_tile_ids))
    total = voltage_self_admittance[..., None] * field_b.astype(jnp.float32) + near_terms
    outgoing = jax.vmap(take_rows)(field_b, interface_tiles_per_level)
    grid = outgoing.reshape(N_ELEC, N_THERM, LEVELS, FACE, TILE_POINT_COUNT, LOAD_REGIMES)
    pieces = []
    for level_bit in range(LEVELS):
        partner = np.arange(N_ELEC) ^ (1 << level_bit)
        pieces.append(grid[partner, :, level_bit])
    incoming = jnp.stack(pieces, axis=2).reshape(unit_count_overall, LEVELS * FACE, TILE_POINT_COUNT, LOAD_REGIMES)
    face_terms = jnp.einsum("gsab,gsbc->gsac", interface_admittance.astype(jnp.float32), incoming.astype(jnp.float32))
    targets = interface_tiles_per_level.reshape(unit_count_overall, LEVELS * FACE)
    return jax.vmap(add_rows)(total, targets, face_terms)


def reference(injected_amperage, voltage_self_admittance, voltage_coupling_tiles, voltage_partner_tile_ids, interface_tiles_per_level, interface_admittance, warmth_receiver_layer, warmth_receiver_tile, warmth_values, warmth_self_coefficient, warmth_coupling_tiles, warmth_partner_tile_ids, layer_boundary_couplings, substance_kind, reference_material_kappas, warmth_storage_per_point):
    unit_count_overall = N_ELEC * N_THERM
    source = injected_amperage.astype(jnp.float32).reshape(unit_count_overall, EB_DEV, TILE_POINT_COUNT, LOAD_REGIMES)
    diag_e = voltage_self_admittance.reshape(unit_count_overall, EB_DEV, TILE_POINT_COUNT)
    near_e = voltage_coupling_tiles.reshape(unit_count_overall, EB_DEV, K_LOC, TILE_POINT_COUNT, TILE_POINT_COUNT)
    conn_e = voltage_partner_tile_ids.reshape(unit_count_overall, EB_DEV, K_LOC)
    sends = interface_tiles_per_level.reshape(unit_count_overall, LEVELS, FACE)
    faces = interface_admittance.reshape(unit_count_overall, LEVELS * FACE, TILE_POINT_COUNT, TILE_POINT_COUNT)
    potential_f = relax_factor * source / diag_e[..., None]
    for sweep_index in range(SWEEPS - 1):
        field_b = potential_f.astype(jnp.bfloat16)
        image = electric_apply(field_b, diag_e, near_e, conn_e, sends, faces)
        potential_f = potential_f + relax_factor * (source - image) / diag_e[..., None]
    voltage_solution = potential_f.astype(jnp.bfloat16)
    current = electric_apply(voltage_solution, diag_e, near_e, conn_e, sends, faces)
    heat = (voltage_solution.astype(jnp.float32) * current).astype(jnp.bfloat16)

    heat_groups = heat.reshape(N_ELEC, N_THERM * EB_DEV, TILE_POINT_COUNT, LOAD_REGIMES)
    owner_groups = warmth_receiver_layer.reshape(N_ELEC, N_THERM * EB_DEV)
    row_groups = warmth_receiver_tile.reshape(N_ELEC, N_THERM * EB_DEV)

    def collect(operands):
        heat_piece, owner_piece, row_piece = operands
        owner_hit = owner_piece[None, None, :] == jnp.arange(N_THERM)[:, None, None]
        row_hit = row_piece[None, None, :] == jnp.arange(UNIT_WARMTH_TILES)[None, :, None]
        selector = (owner_hit & row_hit).astype(jnp.float32)
        return jnp.einsum("tjr,rbc->tjbc", selector, heat_piece.astype(jnp.float32))

    resistive_dissipation = lax.map(collect, (heat_groups, owner_groups, row_groups)).reshape(unit_count_overall, UNIT_WARMTH_TILES, TILE_POINT_COUNT, LOAD_REGIMES)

    warmth_distribution = warmth_values.astype(jnp.float32).reshape(unit_count_overall, UNIT_WARMTH_TILES, TILE_POINT_COUNT, LOAD_REGIMES)
    pass_along = reference_material_kappas[substance_kind].reshape(unit_count_overall, UNIT_WARMTH_TILES, TILE_POINT_COUNT)
    diffusivity_coefficient = pass_along[..., None] * (1.0 + 0.4 * jnp.tanh(warmth_distribution))
    stream_flow_second = (diffusivity_coefficient * warmth_distribution).astype(jnp.bfloat16)
    near_t = warmth_coupling_tiles.reshape(unit_count_overall, UNIT_WARMTH_TILES, K_T, TILE_POINT_COUNT, TILE_POINT_COUNT)
    conn_t = warmth_partner_tile_ids.reshape(unit_count_overall, UNIT_WARMTH_TILES, K_T)
    diag_t = warmth_self_coefficient.reshape(unit_count_overall, UNIT_WARMTH_TILES, TILE_POINT_COUNT)
    warmth_spread_operator = diag_t[..., None] * stream_flow_second.astype(jnp.float32) + lax.map(near_product, (stream_flow_second, near_t, conn_t))
    flux_grid = stream_flow_second.reshape(N_ELEC, N_THERM, UNIT_WARMTH_TILES, TILE_POINT_COUNT, LOAD_REGIMES)
    zero_rim = jnp.zeros((N_ELEC, 1, ZB, TILE_POINT_COUNT, LOAD_REGIMES), jnp.bfloat16)
    below = jnp.concatenate([zero_rim, flux_grid[:, :-1, UNIT_WARMTH_TILES - ZB:]], axis=1)
    above = jnp.concatenate([flux_grid[:, 1:, :ZB], zero_rim], axis=1)
    slab_grid = layer_boundary_couplings.reshape(N_ELEC, N_THERM, 2 * ZB, TILE_POINT_COUNT, TILE_POINT_COUNT).astype(jnp.float32)
    low_terms = jnp.einsum("etzab,etzbc->etzac", slab_grid[:, :, :ZB], below.astype(jnp.float32))
    high_terms = jnp.einsum("etzab,etzbc->etzac", slab_grid[:, :, ZB:], above.astype(jnp.float32))
    warmth_spread_operator = warmth_spread_operator.reshape(N_ELEC, N_THERM, UNIT_WARMTH_TILES, TILE_POINT_COUNT, LOAD_REGIMES)
    warmth_spread_operator = warmth_spread_operator.at[:, :, :ZB].add(low_terms).at[:, :, UNIT_WARMTH_TILES - ZB:].add(high_terms)
    warmth_spread_operator = warmth_spread_operator.reshape(unit_count_overall, UNIT_WARMTH_TILES, TILE_POINT_COUNT, LOAD_REGIMES)
    warmth_storage = warmth_storage_per_point.reshape(unit_count_overall, UNIT_WARMTH_TILES, TILE_POINT_COUNT)
    advanced_warmth_values = warmth_distribution + time_increment * (resistive_dissipation - warmth_spread_operator) / warmth_storage[..., None]
    return voltage_solution.reshape(VOLTAGE_TILES, TILE_POINT_COUNT, LOAD_REGIMES), advanced_warmth_values.reshape(WARMTH_TILES, TILE_POINT_COUNT, LOAD_REGIMES)
```

```python
import functools

import jax
import jax.numpy as jnp
from jax import lax
from jax.experimental import pallas as pl
from jax.experimental.pallas import tpu as pltpu
from jax.sharding import PartitionSpec as P

MESH = pl.DeviceIdType.MESH
F32 = jnp.float32
BF16 = jnp.bfloat16

SWEEPS = 5
RELAX = 0.8
STEP = 0.5
B = 32
N = 64
C = 128
LEVELS = 4
SLOTS = 8
CAP = 8
NZ = 8
K_E = 4
K_T = 3
ALL = B + SLOTS

AT_IDS = 0
AT_SRC = AT_IDS + B * K_E
AT_OUT = AT_SRC + ALL
AT_PACK = AT_OUT + B
AT_TIDS = AT_PACK + NZ * CAP
AT_END = AT_TIDS + B * K_T


def loop(n, step, unroll=1, start=0):
    def one(i, _):
        step(i)
        return 0

    lax.fori_loop(start, n, one, 0, unroll=unroll)


def kernel(
    tab,
    kappas,
    ends,
    diag_e,
    faces,
    diag_t,
    kind,
    storage,
    rims,
    source_h,
    tiles_h,
    warm_h,
    ttiles_h,
    v_out,
    w_out,
    source,
    tiles,
    warm,
    ttiles,
    turn,
    scale,
    diag,
    start0,
    pot,
    field,
    near,
    wide,
    tnear,
    inc,
    coef,
    acc,
    flux,
    halo,
    heat,
    outgo,
    income,
    prefix,
    vbuf,
    ends_in,
    ends_s,
    local_sem,
    ex_send,
    ex_recv,
    halo_send,
    halo_recv,
    ends_send,
    ends_recv,
    heat_send,
    heat_recv,
):
    e = lax.axis_index("elec")
    t = lax.axis_index("therm")

    def copy_in(src, dst, i):
        return pltpu.make_async_copy(src, dst, local_sem.at[i])

    c_source = copy_in(source_h, source, 0)
    c_tiles = copy_in(tiles_h, tiles, 1)
    c_warm = copy_in(warm_h, warm, 2)
    c_ttiles = copy_in(ttiles_h, ttiles, 3)
    for c in (c_source, c_tiles, c_warm, c_ttiles):
        c.start()

    def partner(bit):
        return e + (1 << bit) - 2 * (1 << bit) * (lax.rem(lax.div(e, 1 << bit), 2))

    barrier = pltpu.get_barrier_semaphore()
    for bit in range(LEVELS):
        pl.semaphore_signal(barrier, inc=1, device_id={"elec": partner(bit)}, device_id_type=MESH)
    for o in range(1, NZ):
        pl.semaphore_signal(
            barrier, inc=1, device_id={"therm": lax.rem(t + o, NZ)}, device_id_type=MESH
        )

    def exchange(k, b):
        return pltpu.make_async_remote_copy(
            src_ref=field.at[k, pl.ds(B + 2 * b, 2)],
            dst_ref=inc.at[k, pl.ds(2 * b, 2)],
            send_sem=ex_send.at[k, b],
            recv_sem=ex_recv.at[k, b],
            device_id={"elec": partner(b)},
            device_id_type=MESH,
        )

    def give(src, dst, send, recv, o):
        return pltpu.make_async_remote_copy(
            src_ref=src,
            dst_ref=dst,
            send_sem=send,
            recv_sem=recv,
            device_id={"therm": lax.rem(t + o, NZ)},
            device_id_type=MESH,
        )

    turn[...] = jnp.zeros_like(turn)
    turn[0:B, 0:N] = RELAX / diag_e[...]
    turn[B : 2 * B, 0:N] = diag_e[...]
    c_source.wait()
    flipped = turn[...].T[0:N, :]

    def first(i, cur):
        s = jnp.broadcast_to(cur[:, 0:1], (N, C))
        d = jnp.broadcast_to(cur[:, B : B + 1], (N, C))
        scale[i] = s
        diag[i] = d
        v = s * source[i].astype(F32)
        start0[i] = v
        pot[i] = v
        field[0, i] = v.astype(BF16)
        return pltpu.roll(cur, C - 1, 1)

    lax.fori_loop(0, B, first, flipped, unroll=2)

    def slot_copy(m):
        i = tab[AT_SRC + m]
        field[0, m] = field[0, i]

    loop(ALL, slot_copy, 8, B)
    pl.semaphore_wait(barrier, LEVELS + NZ - 1)
    for b in reversed(range(LEVELS)):
        exchange(0, b).start()

    c_ends = [give(ends.at[lax.rem(t + o, NZ)], ends_in.at[o], ends_send.at[o], ends_recv.at[o], o) for o in range(1, NZ)]
    for c in c_ends:
        c.start()
    ends_in[0] = ends[t]

    def slot_more(m):
        i = tab[AT_SRC + m]
        scale[m] = scale[i]
        diag[m] = diag[i]
        start0[m] = start0[i]
        pot[m] = start0[i]

    loop(ALL, slot_more, 2, B)

    for s in range(SLOTS):
        for q in range(SLOTS):
            same = (tab[AT_SRC + B + s] == tab[AT_SRC + B + q]).astype(F32)
            wide[s, :, q * N : (q + 1) * N] = (faces[q].astype(F32) * same).astype(BF16)

    c_tiles.wait()

    def lay_e(i):
        near[i] = jnp.concatenate([tiles[i, k] for k in range(K_E)], axis=1)

    loop(B, lay_e, 2)

    def product(k, m):
        i = tab[AT_SRC + m]
        rhs = jnp.concatenate(
            [field[k, tab[AT_IDS + i * K_E + q]] for q in range(K_E)], axis=0
        )
        return jnp.dot(near[i], rhs, preferred_element_type=F32)

    def sweep(k):
        def update(m):
            new = pot[m] + start0[m] - RELAX * field[k, m].astype(F32) - scale[m] * product(k, m)
            pot[m] = new
            return new

        loop(ALL, update, 4, B)

        def natural(m):
            field[k + 1, m] = update(m).astype(BF16)

        loop(B, natural, 4)

    def face_terms(k, then):
        for b in range(LEVELS):
            exchange(k, b).wait_recv()
        rhs = inc[k].reshape(SLOTS * N, C)

        def one(s):
            then(s, jnp.dot(wide[s], rhs, preferred_element_type=F32))

        loop(SLOTS, one, 4)

    def finish(k):
        def then(s, g):
            new = pot[B + s] - scale[B + s] * g
            pot[B + s] = new
            field[k + 1, B + s] = new.astype(BF16)

        face_terms(k, then)
        for b in reversed(range(LEVELS)):
            exchange(k + 1, b).start()

    sweep(0)
    finish(0)

    c_up = give(flux.at[pl.ds(B - 2, 2)], halo.at[pl.ds(0, 2)], halo_send.at[0], halo_recv.at[0], 1)
    c_down = give(flux.at[pl.ds(0, 2)], halo.at[pl.ds(2, 2)], halo_send.at[1], halo_recv.at[1], NZ - 1)
    sweep(1)
    c_warm.wait()
    kap = jnp.zeros((B, N), F32)
    for m in range(8):
        kap = kap + jnp.where(kind[...] == m, kappas[m], 0.0)
    turn[0:B, 0:N] = diag_t[...]
    turn[B : 2 * B, 0:N] = kap
    turn[2 * B : 3 * B, 0:N] = STEP / storage[...]
    tflipped = turn[...].T[0:N, :]

    def warmth(i, cur):
        dt = jnp.broadcast_to(cur[:, 0:1], (N, C))
        ka = jnp.broadcast_to(cur[:, B : B + 1], (N, C))
        co = jnp.broadcast_to(cur[:, 2 * B : 2 * B + 1], (N, C))
        w = warm[i].astype(F32)
        fl = (ka * (1.0 + 0.4 * jnp.tanh(w)) * w).astype(BF16)
        flux[i] = fl
        coef[i] = co
        acc[i] = w - co * (dt * fl.astype(F32))
        return pltpu.roll(cur, C - 1, 1)

    lax.fori_loop(0, B, warmth, tflipped, unroll=2)
    c_up.start()
    c_down.start()
    finish(1)
    sweep(2)
    c_ttiles.wait()

    def lay_t(i):
        tnear[i] = jnp.concatenate([ttiles[i, k] for k in range(K_T)], axis=1)

    loop(B, lay_t, 2)
    finish(2)
    sweep(3)

    def conduct(i):
        rhs = jnp.concatenate([flux[tab[AT_TIDS + i * K_T + q]] for q in range(K_T)], axis=0)
        acc[i] = acc[i] - coef[i] * jnp.dot(tnear[i], rhs, preferred_element_type=F32)

    loop(B, conduct, 4)
    finish(3)

    last = SWEEPS - 1

    def slot_current(m):
        pot[m] = diag[m] * field[last, m].astype(F32) + product(last, m)

    loop(ALL, slot_current, 4, B)

    def natural_heat(m):
        f = field[last, m].astype(F32)
        heat[m] = (f * (diag[m] * f + product(last, m))).astype(BF16)

    loop(B, natural_heat, 4)

    def place(i):
        vbuf[i] = field[last, tab[AT_OUT + i]]

    loop(B, place, 4)
    c_v = copy_in(vbuf, v_out, 4)
    c_v.start()

    c_up.wait()
    c_down.wait()
    for z in range(2):
        low = jnp.dot(rims[z], halo[z], preferred_element_type=F32)
        acc[z] = acc[z] - jnp.where(t > 0, 1.0, 0.0) * coef[z] * low
        high = jnp.dot(rims[2 + z], halo[2 + z], preferred_element_type=F32)
        acc[B - 2 + z] = acc[B - 2 + z] - jnp.where(t < NZ - 1, 1.0, 0.0) * coef[B - 2 + z] * high
    for c in c_ends:
        c.wait()
    c_table = pltpu.make_async_copy(ends_in, ends_s, local_sem.at[5])
    c_table.start()
    c_table.wait()

    def slot_heat(s, g):
        heat[B + s] = (field[last, B + s].astype(F32) * (pot[B + s] + g)).astype(BF16)

    face_terms(last, slot_heat)

    order = (4, 3, 5, 2, 6, 1, 7)
    c_heat = {
        o: give(outgo.at[o], income.at[o], heat_send.at[o], heat_recv.at[o], o) for o in order
    }
    for o in order:
        to = lax.rem(t + o, NZ)
        for s in range(CAP):
            outgo[o, s] = heat[tab[AT_PACK + to * CAP + s]]
        c_heat[o].start()
    for s in range(CAP):
        income[0, s] = heat[tab[AT_PACK + t * CAP + s]]

    def collect(o):
        run = jnp.zeros((N, C), F32)
        prefix[0] = run
        for s in range(CAP):
            run = run + income[o, s].astype(F32)
            prefix[s + 1] = run

        def row(j):
            upto = prefix[ends_s[o, 0, j + 1]]
            before = prefix[ends_s[o, 0, j]]
            acc[j] = acc[j] + coef[j] * (upto - before)

        loop(B, row, 2)

    collect(0)
    for o in order:
        c_heat[o].wait_recv()
        collect(o)
    c_w = copy_in(acc, w_out, 6)
    c_w.start()
    for o in order:
        c_heat[o].wait_send()
    for k in range(SWEEPS):
        for b in range(LEVELS):
            exchange(k, b).wait_send()
    c_v.wait()
    c_w.wait()


def tables(conn, sends, owner, row, tconn):
    targets = sends.reshape(-1)
    far = jnp.int32(1000)
    slot = jnp.arange(SLOTS, dtype=jnp.int32)
    block = jnp.arange(B, dtype=jnp.int32)

    def moved(x):
        hit = jnp.min(jnp.where(x[..., None] == targets, B + slot, far), axis=-1)
        return jnp.where(hit < far, hit, x)

    own = owner[:, 0]
    earlier = (row[None, :] < row[:, None]) | (
        (row[None, :] == row[:, None]) & (block[None, :] < block[:, None])
    )
    rank = jnp.sum(((own[None, :] == own[:, None]) & earlier).astype(jnp.int32), axis=1)
    places = own * CAP + rank
    spots = jnp.arange(NZ * CAP, dtype=jnp.int32)
    at = moved(block)
    pack = jnp.sum(jnp.where(places[None, :] == spots[:, None], at[None, :], 0), axis=1)
    tab = jnp.concatenate(
        [moved(conn).reshape(-1), block, targets, at, pack, tconn.reshape(-1)]
    )
    upto = jnp.arange(C, dtype=jnp.int32)
    z = jnp.arange(NZ, dtype=jnp.int32)
    ends = jnp.sum(
        (
            (own[None, None, :] == z[:, None, None]) & (row[None, None, :] < upto[None, :, None])
        ).astype(jnp.int32),
        axis=2,
    )
    return tab, jnp.broadcast_to(ends[:, None, :], (NZ, 8, C))


def body(
    injected_amperage,
    voltage_self_admittance,
    voltage_coupling_tiles,
    voltage_partner_tile_ids,
    interface_tiles_per_level,
    interface_admittance,
    warmth_receiver_layer,
    warmth_receiver_tile,
    warmth_values,
    warmth_self_coefficient,
    warmth_coupling_tiles,
    warmth_partner_tile_ids,
    layer_boundary_couplings,
    substance_kind,
    reference_material_kappas,
    warmth_storage_per_point,
):
    tab, ends = tables(
        voltage_partner_tile_ids,
        interface_tiles_per_level,
        warmth_receiver_layer,
        warmth_receiver_tile,
        warmth_partner_tile_ids,
    )
    smem = pl.BlockSpec(memory_space=pltpu.SMEM)
    vmem = pl.BlockSpec(memory_space=pltpu.VMEM)
    hbm = pl.BlockSpec(memory_space=pl.ANY)
    dma = pltpu.SemaphoreType.DMA
    V = pltpu.VMEM
    return pl.pallas_call(
        kernel,
        out_shape=(
            jax.ShapeDtypeStruct((B, N, C), BF16),
            jax.ShapeDtypeStruct((B, N, C), F32),
        ),
        in_specs=[smem, smem] + [vmem] * 7 + [hbm] * 4,
        out_specs=(hbm, hbm),
        scratch_shapes=[
            V((B, N, C), BF16),
            V((B, K_E, N, N), BF16),
            V((B, N, C), BF16),
            V((B, K_T, N, N), BF16),
            V((C, C), F32),
            V((ALL, N, C), F32),
            V((ALL, N, C), F32),
            V((ALL, N, C), F32),
            V((ALL, N, C), F32),
            V((SWEEPS, ALL, N, C), BF16),
            V((B, N, K_E * N), BF16),
            V((SLOTS, N, SLOTS * N), BF16),
            V((B, N, K_T * N), BF16),
            V((SWEEPS, SLOTS, N, C), BF16),
            V((B, N, C), F32),
            V((B, N, C), F32),
            V((B, N, C), BF16),
            V((4, N, C), BF16),
            V((ALL, N, C), BF16),
            V((NZ, CAP, N, C), BF16),
            V((NZ, CAP, N, C), BF16),
            V((CAP + 1, N, C), F32),
            V((B, N, C), BF16),
            V((NZ, 8, C), jnp.int32),
            pltpu.SMEM((NZ, 8, C), jnp.int32),
            dma((7,)),
            dma((SWEEPS, LEVELS)),
            dma((SWEEPS, LEVELS)),
            dma((2,)),
            dma((2,)),
            dma((NZ,)),
            dma((NZ,)),
            dma((NZ,)),
            dma((NZ,)),
        ],
        compiler_params=pltpu.CompilerParams(
            collective_id=0, has_side_effects=True, vmem_limit_bytes=48 * 1024 * 1024
        ),
    )(
        tab,
        reference_material_kappas,
        ends,
        voltage_self_admittance,
        interface_admittance,
        warmth_self_coefficient,
        substance_kind,
        warmth_storage_per_point,
        layer_boundary_couplings,
        injected_amperage,
        voltage_coupling_tiles,
        warmth_values,
        warmth_coupling_tiles,
    )


def solution(mesh):
    both = ("elec", "therm")

    def split(rank):
        return P(both, *([None] * (rank - 1)))

    return jax.shard_map(
        body,
        mesh=mesh,
        in_specs=(
            split(3),
            split(2),
            split(4),
            split(2),
            split(2),
            split(3),
            split(2),
            split(1),
            split(3),
            split(2),
            split(4),
            split(2),
            split(3),
            split(2),
            P(),
            split(2),
        ),
        out_specs=(split(3), split(3)),
        check_vma=False,
    )
```

```python
import functools

import jax
import jax.numpy as jnp
from jax import lax
from jax.experimental import pallas as pl
from jax.experimental.pallas import tpu as pltpu
from jax.sharding import PartitionSpec as P

MESH = pl.DeviceIdType.MESH
F32 = jnp.float32
BF16 = jnp.bfloat16

SWEEPS = 5
RELAX = 0.8
STEP = 0.5
B = 32
N = 64
C = 128
LEVELS = 4
SLOTS = 8
CAP = 8
NZ = 8
K_E = 4
K_T = 3
ALL = B + SLOTS

ROW_IDS = 0
ROW_TIDS = ROW_IDS + K_E
ROW_OUT = ROW_TIDS + K_T
ROW_PACK = ROW_OUT + 1
ROWS = 16


def loop(n, step, unroll=1, start=0):
    def one(i, _):
        step(i)
        return 0

    lax.fori_loop(start, n, one, 0, unroll=unroll)


def kernel(
    kappas_h,
    conn_h,
    sends_h,
    owner_h,
    row_h,
    tconn_h,
    diag_e_h,
    faces_h,
    diag_t_h,
    kind_h,
    storage_h,
    rims_h,
    source_h,
    tiles_h,
    warm_h,
    ttiles_h,
    v_out,
    acc,
    kappas,
    sends,
    conn,
    owner,
    row,
    tconn,
    diag_e,
    faces,
    diag_t,
    kind,
    storage,
    rims,
    source,
    tiles,
    warm,
    ttiles,
    tab_v,
    tab,
    ends,
    turn,
    iturn,
    scale,
    diag,
    start0,
    pot,
    field,
    near,
    wide,
    tnear,
    inc,
    coef,
    flux,
    halo,
    heat,
    outgo,
    income,
    prefix,
    ends_in,
    ends_s,
    local_sem,
    ex_send,
    ex_recv,
    halo_send,
    halo_recv,
    ends_send,
    ends_recv,
    heat_send,
    heat_recv,
):
    e = lax.axis_index("elec")
    t = lax.axis_index("therm")

    def copy_in(src, dst, i):
        return pltpu.make_async_copy(src, dst, local_sem.at[i])

    pairs = (
        (diag_e_h, diag_e),
        (source_h, source),
        (sends_h, sends),
        (conn_h, conn),
        (tconn_h, tconn),
        (owner_h, owner),
        (row_h, row),
        (faces_h, faces),
        (tiles_h, tiles),
        (warm_h, warm),
        (kappas_h, kappas),
        (kind_h, kind),
        (diag_t_h, diag_t),
        (storage_h, storage),
        (rims_h, rims),
        (ttiles_h, ttiles),
    )
    loads = [copy_in(src, dst, i) for i, (src, dst) in enumerate(pairs)]
    for c in loads:
        c.start()

    def partner(bit):
        return e + (1 << bit) - 2 * (1 << bit) * (lax.rem(lax.div(e, 1 << bit), 2))

    barrier = pltpu.get_barrier_semaphore()
    for bit in range(LEVELS):
        pl.semaphore_signal(barrier, inc=1, device_id={"elec": partner(bit)}, device_id_type=MESH)
    for o in range(1, NZ):
        pl.semaphore_signal(
            barrier, inc=1, device_id={"therm": lax.rem(t + o, NZ)}, device_id_type=MESH
        )

    def exchange(k, b):
        return pltpu.make_async_remote_copy(
            src_ref=field.at[k, pl.ds(B + 2 * b, 2)],
            dst_ref=inc.at[k, pl.ds(2 * b, 2)],
            send_sem=ex_send.at[k, b],
            recv_sem=ex_recv.at[k, b],
            device_id={"elec": partner(b)},
            device_id_type=MESH,
        )

    def give(src, dst, send, recv, o):
        return pltpu.make_async_remote_copy(
            src_ref=src,
            dst_ref=dst,
            send_sem=send,
            recv_sem=recv,
            device_id={"therm": lax.rem(t + o, NZ)},
            device_id_type=MESH,
        )

    turn[...] = jnp.zeros_like(turn)
    loads[0].wait()
    turn[0:B, 0:N] = RELAX / diag_e[...]
    turn[B : 2 * B, 0:N] = diag_e[...]
    loads[1].wait()
    loads[2].wait()
    flipped = turn[...].T[0:N, :]

    def first(i, cur):
        s = jnp.broadcast_to(cur[:, 0:1], (N, C))
        d = jnp.broadcast_to(cur[:, B : B + 1], (N, C))
        scale[i] = s
        diag[i] = d
        v = s * source[i].astype(F32)
        start0[i] = v
        pot[i] = v
        field[0, i] = v.astype(BF16)
        return pltpu.roll(cur, C - 1, 1)

    lax.fori_loop(0, B, first, flipped, unroll=2)

    tiles_of_slots = [sends[s % 2, s // 2] for s in range(SLOTS)]
    for s in range(SLOTS):
        field[0, B + s] = field[0, tiles_of_slots[s]]
    pl.semaphore_wait(barrier, LEVELS + NZ - 1)
    for b in reversed(range(LEVELS)):
        exchange(0, b).start()

    def moved(x):
        hit = x
        for s in reversed(range(SLOTS)):
            hit = jnp.where(x == tiles_of_slots[s], B + s, hit)
        return hit

    for i in range(3, 7):
        loads[i].wait()
    tab_v[...] = jnp.zeros_like(tab_v)
    tab_v[ROW_IDS : ROW_IDS + K_E, 0:B] = moved(conn[...])
    tab_v[ROW_TIDS : ROW_TIDS + K_T, 0:B] = tconn[...]
    tab_v[ROW_OUT : ROW_OUT + 1, 0:B] = moved(lax.broadcasted_iota(jnp.int32, (1, B), 1))
    iturn[...] = jnp.zeros_like(iturn)
    iturn[0:1, 0:B] = owner[...]
    iturn[1:2, 0:B] = row[...]
    columns = iturn[...].T
    block = lax.broadcasted_iota(jnp.int32, (B, C), 0)
    lane = lax.broadcasted_iota(jnp.int32, (B, C), 1)
    own_c = jnp.broadcast_to(columns[0:B, 0:1], (B, C))
    row_c = jnp.broadcast_to(columns[0:B, 1:2], (B, C))
    own_r = jnp.broadcast_to(iturn[0:1, :], (B, C))
    row_r = jnp.broadcast_to(iturn[1:2, :], (B, C))
    earlier = (own_r == own_c) & (lane < B) & (row_r * B + lane < row_c * B + block)
    rank = jnp.sum(jnp.where(earlier, 1.0, 0.0), axis=1, keepdims=True).astype(jnp.int32)
    place_c = own_c * CAP + jnp.broadcast_to(rank, (B, C))
    packed = jnp.where(place_c == lane, moved(block), 0)
    tab_v[ROW_PACK : ROW_PACK + 1, :] = jnp.clip(
        jnp.sum(packed, axis=0, keepdims=True), 0, ALL - 1
    )
    c_tab = copy_in(tab_v, tab, 16)
    c_tab.start()

    for z in range(NZ):
        before = jnp.where((own_c == z) & (row_c < lane), 1, 0)
        ends[z, 0:1, :] = jnp.clip(jnp.sum(before, axis=0, keepdims=True), 0, CAP)
        ends[z, 1:8, :] = jnp.zeros((7, C), jnp.int32)
    c_ends = [
        give(ends.at[lax.rem(t + o, NZ)], ends_in.at[o], ends_send.at[o], ends_recv.at[o], o)
        for o in range(1, NZ)
    ]
    for c in c_ends:
        c.start()
    ends_in[0] = ends[t]

    for s in range(SLOTS):
        i = tiles_of_slots[s]
        scale[B + s] = scale[i]
        diag[B + s] = diag[i]
        start0[B + s] = start0[i]
        pot[B + s] = start0[i]

    loads[7].wait()
    for s in range(SLOTS):
        for q in range(SLOTS):
            same = (tiles_of_slots[s] == tiles_of_slots[q]).astype(F32)
            wide[s, :, q * N : (q + 1) * N] = (faces[q].astype(F32) * same).astype(BF16)

    loads[8].wait()

    def lay_e(i):
        near[i] = jnp.concatenate([tiles[i, k] for k in range(K_E)], axis=1)

    loop(B, lay_e, 2)
    c_tab.wait()

    def product(k, i):
        rhs = jnp.concatenate([field[k, tab[ROW_IDS + q, i]] for q in range(K_E)], axis=0)
        return jnp.dot(near[i], rhs, preferred_element_type=F32)

    def sweep(k):
        def update(m, i):
            new = pot[m] + start0[m] - RELAX * field[k, m].astype(F32) - scale[m] * product(k, i)
            pot[m] = new
            return new

        for s in range(SLOTS):
            update(B + s, tiles_of_slots[s])

        def natural(m):
            field[k + 1, m] = update(m, m).astype(BF16)

        loop(B, natural, 4)

    def face_terms(k, then):
        for b in range(LEVELS):
            exchange(k, b).wait_recv()
        rhs = inc[k].reshape(SLOTS * N, C)

        def one(s):
            then(s, jnp.dot(wide[s], rhs, preferred_element_type=F32))

        loop(SLOTS, one, 4)

    def finish(k):
        def then(s, g):
            new = pot[B + s] - scale[B + s] * g
            pot[B + s] = new
            field[k + 1, B + s] = new.astype(BF16)

        face_terms(k, then)
        for b in reversed(range(LEVELS)):
            exchange(k + 1, b).start()

    sweep(0)
    finish(0)

    c_up = give(flux.at[pl.ds(B - 2, 2)], halo.at[pl.ds(0, 2)], halo_send.at[0], halo_recv.at[0], 1)
    c_down = give(flux.at[pl.ds(0, 2)], halo.at[pl.ds(2, 2)], halo_send.at[1], halo_recv.at[1], NZ - 1)
    sweep(1)
    for i in range(9, 15):
        loads[i].wait()
    kap = jnp.zeros((B, N), F32)
    for m in range(8):
        kap = kap + jnp.where(kind[...] == m, kappas[m], 0.0)
    turn[0:B, 0:N] = diag_t[...]
    turn[B : 2 * B, 0:N] = kap
    turn[2 * B : 3 * B, 0:N] = STEP / storage[...]
    tflipped = turn[...].T[0:N, :]

    def warmth(i, cur):
        dt = jnp.broadcast_to(cur[:, 0:1], (N, C))
        ka = jnp.broadcast_to(cur[:, B : B + 1], (N, C))
        co = jnp.broadcast_to(cur[:, 2 * B : 2 * B + 1], (N, C))
        w = warm[i].astype(F32)
        fl = (ka * (1.0 + 0.4 * jnp.tanh(w)) * w).astype(BF16)
        flux[i] = fl
        coef[i] = co
        acc[i] = w - co * (dt * fl.astype(F32))
        return pltpu.roll(cur, C - 1, 1)

    lax.fori_loop(0, B, warmth, tflipped, unroll=2)
    c_up.start()
    c_down.start()
    finish(1)
    sweep(2)
    loads[15].wait()

    def lay_t(i):
        tnear[i] = jnp.concatenate([ttiles[i, k] for k in range(K_T)], axis=1)

    loop(B, lay_t, 2)
    finish(2)
    sweep(3)

    def conduct(i):
        rhs = jnp.concatenate([flux[tab[ROW_TIDS + q, i]] for q in range(K_T)], axis=0)
        acc[i] = acc[i] - coef[i] * jnp.dot(tnear[i], rhs, preferred_element_type=F32)

    loop(B, conduct, 4)
    finish(3)

    last = SWEEPS - 1

    for s in range(SLOTS):
        pot[B + s] = diag[B + s] * field[last, B + s].astype(F32) + product(last, tiles_of_slots[s])

    def natural_heat(m):
        f = field[last, m].astype(F32)
        heat[m] = (f * (diag[m] * f + product(last, m))).astype(BF16)

    loop(B, natural_heat, 4)

    def place(i):
        v_out[i] = field[last, tab[ROW_OUT, i]]

    loop(B, place, 4)

    c_up.wait()
    c_down.wait()
    for z in range(2):
        low = jnp.dot(rims[z], halo[z], preferred_element_type=F32)
        acc[z] = acc[z] - jnp.where(t > 0, 1.0, 0.0) * coef[z] * low
        high = jnp.dot(rims[2 + z], halo[2 + z], preferred_element_type=F32)
        acc[B - 2 + z] = acc[B - 2 + z] - jnp.where(t < NZ - 1, 1.0, 0.0) * coef[B - 2 + z] * high
    for c in c_ends:
        c.wait()
    c_table = pltpu.make_async_copy(ends_in, ends_s, local_sem.at[17])
    c_table.start()
    c_table.wait()

    def slot_heat(s, g):
        heat[B + s] = (field[last, B + s].astype(F32) * (pot[B + s] + g)).astype(BF16)

    face_terms(last, slot_heat)

    order = (4, 3, 5, 2, 6, 1, 7)
    c_heat = {
        o: give(outgo.at[o], income.at[o], heat_send.at[o], heat_recv.at[o], o) for o in order
    }
    for o in order:
        to = lax.rem(t + o, NZ)
        for s in range(CAP):
            outgo[o, s] = heat[tab[ROW_PACK, to * CAP + s]]
        c_heat[o].start()
    for s in range(CAP):
        income[0, s] = heat[tab[ROW_PACK, t * CAP + s]]

    def collect(o):
        run = jnp.zeros((N, C), F32)
        prefix[0] = run
        for s in range(CAP):
            run = run + income[o, s].astype(F32)
            prefix[s + 1] = run

        def row(j):
            upto = prefix[ends_s[o, 0, j + 1]]
            before = prefix[ends_s[o, 0, j]]
            acc[j] = acc[j] + coef[j] * (upto - before)

        loop(B, row, 2)

    collect(0)
    for o in order:
        c_heat[o].wait_recv()
        collect(o)
    for o in order:
        c_heat[o].wait_send()
    for k in range(SWEEPS):
        for b in range(LEVELS):
            exchange(k, b).wait_send()


def body(
    injected_amperage,
    voltage_self_admittance,
    voltage_coupling_tiles,
    voltage_partner_tile_ids,
    interface_tiles_per_level,
    interface_admittance,
    warmth_receiver_layer,
    warmth_receiver_tile,
    warmth_values,
    warmth_self_coefficient,
    warmth_coupling_tiles,
    warmth_partner_tile_ids,
    layer_boundary_couplings,
    substance_kind,
    reference_material_kappas,
    warmth_storage_per_point,
):
    vmem = pl.BlockSpec(memory_space=pltpu.VMEM)
    hbm = pl.BlockSpec(memory_space=pltpu.HBM)
    dma = pltpu.SemaphoreType.DMA
    V = pltpu.VMEM
    I32 = jnp.int32
    return pl.pallas_call(
        kernel,
        out_shape=(
            jax.ShapeDtypeStruct((B, N, C), BF16),
            jax.ShapeDtypeStruct((B, N, C), F32),
        ),
        in_specs=[hbm] * 16,
        out_specs=(vmem, vmem),
        scratch_shapes=[
            pltpu.SMEM((8,), F32),
            pltpu.SMEM((2, LEVELS), I32),
            V((K_E, B), I32),
            V((1, B), I32),
            V((1, B), I32),
            V((K_T, B), I32),
            V((B, N), F32),
            V((SLOTS, N, N), BF16),
            V((B, N), F32),
            V((B, N), I32),
            V((B, N), F32),
            V((4, N, N), BF16),
            V((B, N, C), BF16),
            V((B, K_E, N, N), BF16),
            V((B, N, C), BF16),
            V((B, K_T, N, N), BF16),
            V((ROWS, C), I32),
            pltpu.SMEM((ROWS, C), I32),
            V((NZ, 8, C), I32),
            V((C, C), F32),
            V((C, C), I32),
            V((ALL, N, C), F32),
            V((ALL, N, C), F32),
            V((ALL, N, C), F32),
            V((ALL, N, C), F32),
            V((SWEEPS, ALL, N, C), BF16),
            V((B, N, K_E * N), BF16),
            V((SLOTS, N, SLOTS * N), BF16),
            V((B, N, K_T * N), BF16),
            V((SWEEPS, SLOTS, N, C), BF16),
            V((B, N, C), F32),
            V((B, N, C), BF16),
            V((4, N, C), BF16),
            V((ALL, N, C), BF16),
            V((NZ, CAP, N, C), BF16),
            V((NZ, CAP, N, C), BF16),
            V((CAP + 1, N, C), F32),
            V((NZ, 8, C), I32),
            pltpu.SMEM((NZ, 8, C), I32),
            dma((18,)),
            dma((SWEEPS, LEVELS)),
            dma((SWEEPS, LEVELS)),
            dma((2,)),
            dma((2,)),
            dma((NZ,)),
            dma((NZ,)),
            dma((NZ,)),
            dma((NZ,)),
        ],
        compiler_params=pltpu.CompilerParams(
            collective_id=0, has_side_effects=True, vmem_limit_bytes=63 * 1024 * 1024
        ),
    )(
        reference_material_kappas,
        voltage_partner_tile_ids.T,
        interface_tiles_per_level.T,
        warmth_receiver_layer.T,
        warmth_receiver_tile.reshape(1, B),
        warmth_partner_tile_ids.T,
        voltage_self_admittance,
        interface_admittance,
        warmth_self_coefficient,
        substance_kind,
        warmth_storage_per_point,
        layer_boundary_couplings,
        injected_amperage,
        voltage_coupling_tiles,
        warmth_values,
        warmth_coupling_tiles,
    )


def solution(mesh):
    both = ("elec", "therm")

    def split(rank):
        return P(both, *([None] * (rank - 1)))

    return jax.shard_map(
        body,
        mesh=mesh,
        in_specs=(
            split(3),
            split(2),
            split(4),
            split(2),
            split(2),
            split(3),
            split(2),
            split(1),
            split(3),
            split(2),
            split(4),
            split(2),
            split(3),
            split(2),
            P(),
            split(2),
        ),
        out_specs=(split(3), split(3)),
        check_vma=False,
    )
```

```python
import functools

import jax
import jax.numpy as jnp
from jax import lax
from jax.experimental import pallas as pl
from jax.experimental.pallas import tpu as pltpu
from jax.sharding import PartitionSpec as P

MESH = pl.DeviceIdType.MESH
F32 = jnp.float32
BF16 = jnp.bfloat16

SWEEPS = 5
RELAX = 0.8
STEP = 0.5
B = 32
N = 64
C = 128
LEVELS = 4
SLOTS = 8
CAP = 8
NZ = 8
K_E = 4
K_T = 3
ALL = B + SLOTS

ROW_IDS = 0
ROW_TIDS = ROW_IDS + K_E
ROW_OUT = ROW_TIDS + K_T
ROW_PACK = ROW_OUT + 1
ROWS = 16
GROUP = 16
PIECES = 4


def grouped(n, size, read, write):
    def one(g, _):
        at = [g * size + u for u in range(size)]
        got = [read(m) for m in at]
        for m, x in zip(at, got):
            write(m, x)
        return 0

    lax.fori_loop(0, n // size, one, 0)


def kernel(
    kappas_h,
    conn_h,
    sends_h,
    owner_h,
    row_h,
    tconn_h,
    diag_e_h,
    faces_h,
    diag_t_h,
    kind_h,
    storage_h,
    rims_h,
    source_h,
    tiles_h,
    warm_h,
    ttiles_h,
    v_h,
    w_h,
    kappas,
    sends,
    conn,
    owner,
    row,
    tconn,
    diag_e,
    faces,
    diag_t,
    kind,
    storage,
    rims,
    source,
    tiles,
    warm,
    ttiles,
    tab_v,
    tab,
    ends,
    turn,
    iturn,
    scale,
    diag,
    start0,
    pot,
    field0,
    field1,
    field2,
    field3,
    field4,
    part,
    near,
    wide,
    tnear,
    inc,
    coef,
    flux,
    halo,
    heat,
    outgo,
    income,
    prefix,
    acc,
    v_out,
    ends_in,
    ends_s,
    local_sem,
    ex_send,
    ex_recv,
    halo_send,
    halo_recv,
    ends_send,
    ends_recv,
    heat_send,
    heat_recv,
):
    e = lax.axis_index("elec")
    t = lax.axis_index("therm")
    field = (field0, field1, field2, field3, field4)
    last = SWEEPS - 1

    def copy_in(src, dst, i):
        return pltpu.make_async_copy(src, dst, local_sem.at[i])

    pairs = (
        (diag_e_h, diag_e),
        (source_h, source),
        (sends_h, sends),
        (conn_h, conn),
        (tconn_h, tconn),
        (owner_h, owner),
        (row_h, row),
        (faces_h, faces),
        (tiles_h, tiles),
        (warm_h, warm),
        (kappas_h, kappas),
        (kind_h, kind),
        (diag_t_h, diag_t),
        (storage_h, storage),
        (rims_h, rims),
        (ttiles_h, ttiles),
    )
    loads = [copy_in(src, dst, i) for i, (src, dst) in enumerate(pairs)]
    for c in loads:
        c.start()

    def partner(bit):
        return e + (1 << bit) - 2 * (1 << bit) * (lax.rem(lax.div(e, 1 << bit), 2))

    barrier = pltpu.get_barrier_semaphore()
    for bit in range(LEVELS):
        pl.semaphore_signal(barrier, inc=1, device_id={"elec": partner(bit)}, device_id_type=MESH)
    for o in range(1, NZ):
        pl.semaphore_signal(
            barrier, inc=1, device_id={"therm": lax.rem(t + o, NZ)}, device_id_type=MESH
        )

    def exchange(k, b):
        return pltpu.make_async_remote_copy(
            src_ref=field[k].at[pl.ds(B + 2 * b, 2)],
            dst_ref=inc.at[k, pl.ds(2 * b, 2)],
            send_sem=ex_send.at[k, b],
            recv_sem=ex_recv.at[k, b],
            device_id={"elec": partner(b)},
            device_id_type=MESH,
        )

    def give(src, dst, send, recv, o):
        return pltpu.make_async_remote_copy(
            src_ref=src,
            dst_ref=dst,
            send_sem=send,
            recv_sem=recv,
            device_id={"therm": lax.rem(t + o, NZ)},
            device_id_type=MESH,
        )

    turn[...] = jnp.zeros_like(turn)
    loads[0].wait()
    turn[0:B, 0:N] = RELAX / diag_e[...]
    turn[B : 2 * B, 0:N] = diag_e[...]
    flipped = turn[...].T[0:N, :]
    loads[1].wait()
    loads[2].wait()
    tiles_of_slots = [sends[s % 2, s // 2] for s in range(SLOTS)]
    spot = lax.broadcasted_iota(jnp.int32, (N, C), 1)

    def column(x, i):
        return jnp.broadcast_to(
            jnp.sum(jnp.where(spot == i, x, 0.0), axis=1, keepdims=True), (N, C)
        )

    for s in range(SLOTS):
        i = tiles_of_slots[s]
        sc = column(flipped, i)
        v = sc * source[i].astype(F32)
        scale[B + s] = sc
        start0[B + s] = v
        pot[B + s] = v
        field0[B + s] = v.astype(BF16)
    pl.semaphore_wait(barrier, LEVELS + NZ - 1)
    for b in reversed(range(LEVELS)):
        exchange(0, b).start()

    def first(g, cur):
        got = []
        for u in range(8):
            i = g * 8 + u
            sc = jnp.broadcast_to(cur[:, u : u + 1], (N, C))
            d = jnp.broadcast_to(cur[:, B + u : B + u + 1], (N, C))
            got.append((i, sc, d, sc * source[i].astype(F32)))
        for i, sc, d, v in got:
            scale[i] = sc
            diag[i] = d
            start0[i] = v
            pot[i] = v
            field0[i] = v.astype(BF16)
        return pltpu.roll(cur, C - 8, 1)

    lax.fori_loop(0, B // 8, first, flipped)
    for s in range(SLOTS):
        diag[B + s] = column(flipped, tiles_of_slots[s] + B)

    def moved(x):
        hit = x
        for s in reversed(range(SLOTS)):
            hit = jnp.where(x == tiles_of_slots[s], B + s, hit)
        return hit

    for i in range(3, 7):
        loads[i].wait()
    tab_v[...] = jnp.zeros_like(tab_v)
    tab_v[ROW_IDS : ROW_IDS + K_E, 0:B] = moved(conn[...])
    tab_v[ROW_TIDS : ROW_TIDS + K_T, 0:B] = tconn[...]
    tab_v[ROW_OUT : ROW_OUT + 1, 0:B] = moved(lax.broadcasted_iota(jnp.int32, (1, B), 1))
    iturn[...] = jnp.zeros_like(iturn)
    iturn[0:1, 0:B] = owner[...]
    iturn[1:2, 0:B] = row[...]
    columns = iturn[...].T
    block = lax.broadcasted_iota(jnp.int32, (B, C), 0)
    lane = lax.broadcasted_iota(jnp.int32, (B, C), 1)
    own_c = jnp.broadcast_to(columns[0:B, 0:1], (B, C))
    row_c = jnp.broadcast_to(columns[0:B, 1:2], (B, C))
    own_r = jnp.broadcast_to(iturn[0:1, :], (B, C))
    row_r = jnp.broadcast_to(iturn[1:2, :], (B, C))
    earlier = (own_r == own_c) & (lane < B) & (row_r * B + lane < row_c * B + block)
    rank = jnp.sum(jnp.where(earlier, 1.0, 0.0), axis=1, keepdims=True).astype(jnp.int32)
    place_c = own_c * CAP + jnp.broadcast_to(rank, (B, C))
    packed = jnp.where(place_c == lane, moved(block), 0)
    tab_v[ROW_PACK : ROW_PACK + 1, :] = jnp.clip(
        jnp.sum(packed, axis=0, keepdims=True), 0, ALL - 1
    )
    c_tab = copy_in(tab_v, tab, 16)
    c_tab.start()

    for z in range(NZ):
        before = jnp.where((own_c == z) & (row_c < lane), 1, 0)
        ends[z, 0:1, :] = jnp.clip(jnp.sum(before, axis=0, keepdims=True), 0, CAP)
        ends[z, 1:8, :] = jnp.zeros((7, C), jnp.int32)
    c_ends = [
        give(ends.at[lax.rem(t + o, NZ)], ends_in.at[o], ends_send.at[o], ends_recv.at[o], o)
        for o in range(1, NZ)
    ]
    for c in c_ends:
        c.start()
    ends_in[0] = ends[t]

    loads[7].wait()
    for s in range(SLOTS):
        for q in range(SLOTS):
            same = (tiles_of_slots[s] == tiles_of_slots[q]).astype(F32)
            wide[s * N : (s + 1) * N, q * N : (q + 1) * N] = (faces[q].astype(F32) * same).astype(BF16)

    loads[8].wait()

    grouped(
        B,
        8,
        lambda i: jnp.concatenate([tiles[i, k] for k in range(K_E)], axis=1),
        lambda i, x: near.__setitem__(i, x),
    )
    c_tab.wait()

    def product(k, i):
        rhs = jnp.concatenate([field[k][tab[ROW_IDS + q, i]] for q in range(K_E)], axis=0)
        return jnp.dot(near[i], rhs, preferred_element_type=F32)

    def sweep(k):
        def update(m, i):
            return pot[m] + start0[m] - RELAX * field[k][m].astype(F32) - scale[m] * product(k, i)

        got = [update(B + s, tiles_of_slots[s]) for s in range(SLOTS)]
        for s in range(SLOTS):
            pot[B + s] = got[s]

        def store(m, new):
            pot[m] = new
            field[k + 1][m] = new.astype(BF16)

        grouped(B, GROUP, lambda m: update(m, m), store)

    EARLY = (SLOTS - 2) * N

    def face_terms(k, then):
        for b in range(LEVELS - 1):
            exchange(k, b).wait_recv()
        part[...] = jnp.dot(
            wide[:, 0:EARLY], inc[k, 0 : SLOTS - 2].reshape(EARLY, C), preferred_element_type=F32
        )
        exchange(k, LEVELS - 1).wait_recv()
        total = part[...] + jnp.dot(
            wide[:, EARLY:], inc[k, SLOTS - 2 :].reshape(2 * N, C), preferred_element_type=F32
        )
        for s in range(SLOTS):
            then(s, total[s * N : (s + 1) * N])

    def finish(k):
        def then(s, g):
            new = pot[B + s] - scale[B + s] * g
            pot[B + s] = new
            field[k + 1][B + s] = new.astype(BF16)

        face_terms(k, then)
        for b in reversed(range(LEVELS)):
            exchange(k + 1, b).start()

    sweep(0)
    finish(0)

    c_up = give(flux.at[pl.ds(B - 2, 2)], halo.at[pl.ds(0, 2)], halo_send.at[0], halo_recv.at[0], 1)
    c_down = give(flux.at[pl.ds(0, 2)], halo.at[pl.ds(2, 2)], halo_send.at[1], halo_recv.at[1], NZ - 1)
    sweep(1)
    for i in range(9, 15):
        loads[i].wait()
    kap = jnp.zeros((B, N), F32)
    for m in range(8):
        kap = kap + jnp.where(kind[...] == m, kappas[m], 0.0)
    turn[0:B, 0:N] = diag_t[...]
    turn[B : 2 * B, 0:N] = kap
    turn[2 * B : 3 * B, 0:N] = STEP / storage[...]
    tflipped = turn[...].T[0:N, :]

    def warmth(g, cur):
        got = []
        for u in range(8):
            i = g * 8 + u
            dt = jnp.broadcast_to(cur[:, u : u + 1], (N, C))
            ka = jnp.broadcast_to(cur[:, B + u : B + u + 1], (N, C))
            co = jnp.broadcast_to(cur[:, 2 * B + u : 2 * B + u + 1], (N, C))
            w = warm[i].astype(F32)
            fl = (ka * (1.0 + 0.4 * jnp.tanh(w)) * w).astype(BF16)
            got.append((i, fl, co, w - co * (dt * fl.astype(F32))))
        for i, fl, co, x in got:
            flux[i] = fl
            coef[i] = co
            acc[i] = x
        return pltpu.roll(cur, C - 8, 1)

    lax.fori_loop(0, B // 8, warmth, tflipped)
    c_up.start()
    c_down.start()
    finish(1)
    sweep(2)
    loads[15].wait()

    grouped(
        B,
        8,
        lambda i: jnp.concatenate([ttiles[i, k] for k in range(K_T)], axis=1),
        lambda i, x: tnear.__setitem__(i, x),
    )
    finish(2)
    sweep(3)

    def conduct(i):
        rhs = jnp.concatenate([flux[tab[ROW_TIDS + q, i]] for q in range(K_T)], axis=0)
        return acc[i] - coef[i] * jnp.dot(tnear[i], rhs, preferred_element_type=F32)

    grouped(B, GROUP, conduct, lambda i, x: acc.__setitem__(i, x))
    finish(3)

    got = [
        diag[B + s] * field4[B + s].astype(F32) + product(last, tiles_of_slots[s])
        for s in range(SLOTS)
    ]
    for s in range(SLOTS):
        pot[B + s] = got[s]

    def natural_heat(m):
        f = field4[m].astype(F32)
        return (f * (diag[m] * f + product(last, m))).astype(BF16)

    grouped(B, GROUP, natural_heat, lambda m, x: heat.__setitem__(m, x))
    grouped(B, 8, lambda i: field4[tab[ROW_OUT, i]], lambda i, x: v_out.__setitem__(i, x))
    c_v = copy_in(v_out, v_h, 18)
    c_v.start()

    c_up.wait()
    c_down.wait()
    for z in range(2):
        low = jnp.dot(rims[z], halo[z], preferred_element_type=F32)
        acc[z] = acc[z] - jnp.where(t > 0, 1.0, 0.0) * coef[z] * low
        high = jnp.dot(rims[2 + z], halo[2 + z], preferred_element_type=F32)
        acc[B - 2 + z] = acc[B - 2 + z] - jnp.where(t < NZ - 1, 1.0, 0.0) * coef[B - 2 + z] * high
    for c in c_ends:
        c.wait()
    c_table = pltpu.make_async_copy(ends_in, ends_s, local_sem.at[17])
    c_table.start()
    c_table.wait()

    def slot_heat(s, g):
        heat[B + s] = (field4[B + s].astype(F32) * (pot[B + s] + g)).astype(BF16)

    face_terms(last, slot_heat)

    order = (4, 3, 5, 2, 6, 1, 7)
    c_heat = {
        o: give(outgo.at[o], income.at[o], heat_send.at[o], heat_recv.at[o], o) for o in order
    }
    for o in order:
        to = lax.rem(t + o, NZ)
        for s in range(CAP):
            outgo[o, s] = heat[tab[ROW_PACK, to * CAP + s]]
        c_heat[o].start()
    for s in range(CAP):
        income[0, s] = heat[tab[ROW_PACK, t * CAP + s]]

    def collect(o):
        run = jnp.zeros((N, C), F32)
        prefix[0] = run
        for s in range(CAP):
            run = run + income[o, s].astype(F32)
            prefix[s + 1] = run

        def row(j):
            upto = prefix[ends_s[o, 0, j + 1]]
            before = prefix[ends_s[o, 0, j]]
            return acc[j] + coef[j] * (upto - before)

        grouped(B, 4, row, lambda j, x: acc.__setitem__(j, x))

    collect(0)
    for o in order:
        c_heat[o].wait_recv()
        collect(o)
    c_w = copy_in(acc, w_h, 19)
    c_w.start()
    for o in order:
        c_heat[o].wait_send()
    for k in range(SWEEPS):
        for b in range(LEVELS):
            exchange(k, b).wait_send()
    c_v.wait()
    c_w.wait()


def hand_over(v_h, w_h, v_out, w_out, v_mid, w_mid, sem_in, sem_out):
    size = B // PIECES
    ways = []
    for i in range(PIECES):
        piece = pl.ds(i * size, size)
        ways.append((w_h.at[piece], w_mid.at[piece], w_out.at[piece], 0, i))
        ways.append((v_h.at[piece], v_mid.at[piece], v_out.at[piece], 1, i))
    ins = [pltpu.make_async_copy(a, b, sem_in.at[r, i]) for a, b, c, r, i in ways]
    outs = [pltpu.make_async_copy(b, c, sem_out.at[r, i]) for a, b, c, r, i in ways]
    for c in ins:
        c.start()
    for c, d in zip(ins, outs):
        c.wait()
        d.start()
    for d in outs:
        d.wait()


def body(
    injected_amperage,
    voltage_self_admittance,
    voltage_coupling_tiles,
    voltage_partner_tile_ids,
    interface_tiles_per_level,
    interface_admittance,
    warmth_receiver_layer,
    warmth_receiver_tile,
    warmth_values,
    warmth_self_coefficient,
    warmth_coupling_tiles,
    warmth_partner_tile_ids,
    layer_boundary_couplings,
    substance_kind,
    reference_material_kappas,
    warmth_storage_per_point,
):
    hbm = pl.BlockSpec(memory_space=pltpu.HBM)
    dma = pltpu.SemaphoreType.DMA
    V = pltpu.VMEM
    I32 = jnp.int32
    shapes = (
        jax.ShapeDtypeStruct((B, N, C), BF16),
        jax.ShapeDtypeStruct((B, N, C), F32),
    )
    v, w = pl.pallas_call(
        kernel,
        out_shape=shapes,
        in_specs=[hbm] * 16,
        out_specs=(hbm, hbm),
        scratch_shapes=[
            pltpu.SMEM((8,), F32),
            pltpu.SMEM((2, LEVELS), I32),
            V((K_E, B), I32),
            V((1, B), I32),
            V((1, B), I32),
            V((K_T, B), I32),
            V((B, N), F32),
            V((SLOTS, N, N), BF16),
            V((B, N), F32),
            V((B, N), I32),
            V((B, N), F32),
            V((4, N, N), BF16),
            V((B, N, C), BF16),
            V((B, K_E, N, N), BF16),
            V((B, N, C), BF16),
            V((B, K_T, N, N), BF16),
            V((ROWS, C), I32),
            pltpu.SMEM((ROWS, C), I32),
            V((NZ, 8, C), I32),
            V((C, C), F32),
            V((C, C), I32),
            V((ALL, N, C), F32),
            V((ALL, N, C), F32),
            V((ALL, N, C), F32),
            V((ALL, N, C), F32),
            V((ALL, N, C), BF16),
            V((ALL, N, C), BF16),
            V((ALL, N, C), BF16),
            V((ALL, N, C), BF16),
            V((ALL, N, C), BF16),
            V((SLOTS * N, C), F32),
            V((B, N, K_E * N), BF16),
            V((SLOTS * N, SLOTS * N), BF16),
            V((B, N, K_T * N), BF16),
            V((SWEEPS, SLOTS, N, C), BF16),
            V((B, N, C), F32),
            V((B, N, C), BF16),
            V((4, N, C), BF16),
            V((ALL, N, C), BF16),
            V((NZ, CAP, N, C), BF16),
            V((NZ, CAP, N, C), BF16),
            V((CAP + 1, N, C), F32),
            V((B, N, C), F32),
            V((B, N, C), BF16),
            V((NZ, 8, C), I32),
            pltpu.SMEM((NZ, 8, C), I32),
            dma((20,)),
            dma((SWEEPS, LEVELS)),
            dma((SWEEPS, LEVELS)),
            dma((2,)),
            dma((2,)),
            dma((NZ,)),
            dma((NZ,)),
            dma((NZ,)),
            dma((NZ,)),
        ],
        compiler_params=pltpu.CompilerParams(
            collective_id=0, has_side_effects=True, vmem_limit_bytes=63 * 1024 * 1024
        ),
    )(
        reference_material_kappas,
        voltage_partner_tile_ids.T,
        interface_tiles_per_level.T,
        warmth_receiver_layer.T,
        warmth_receiver_tile.reshape(1, B),
        warmth_partner_tile_ids.T,
        voltage_self_admittance,
        interface_admittance,
        warmth_self_coefficient,
        substance_kind,
        warmth_storage_per_point,
        layer_boundary_couplings,
        injected_amperage,
        voltage_coupling_tiles,
        warmth_values,
        warmth_coupling_tiles,
    )
    return pl.pallas_call(
        hand_over,
        out_shape=shapes,
        in_specs=[hbm, hbm],
        out_specs=(hbm, hbm),
        scratch_shapes=[V((B, N, C), BF16), V((B, N, C), F32), dma((2, PIECES)), dma((2, PIECES))],
        compiler_params=pltpu.CompilerParams(vmem_limit_bytes=63 * 1024 * 1024),
    )(v, w)


def solution(mesh):
    both = ("elec", "therm")

    def split(rank):
        return P(both, *([None] * (rank - 1)))

    return jax.shard_map(
        body,
        mesh=mesh,
        in_specs=(
            split(3),
            split(2),
            split(4),
            split(2),
            split(2),
            split(3),
            split(2),
            split(1),
            split(3),
            split(2),
            split(4),
            split(2),
            split(3),
            split(2),
            P(),
            split(2),
        ),
        out_specs=(split(3), split(3)),
        check_vma=False,
    )
```

```python
import functools

import jax
import jax.numpy as jnp
from jax import lax
from jax.experimental import pallas as pl
from jax.experimental.pallas import tpu as pltpu
from jax.sharding import PartitionSpec as P

MESH = pl.DeviceIdType.MESH
F32 = jnp.float32
BF16 = jnp.bfloat16

SWEEPS = 5
RELAX = 0.8
STEP = 0.5
B = 32
N = 64
C = 128
LEVELS = 4
SLOTS = 8
CAP = 8
NZ = 8
K_E = 4
K_T = 3
ALL = B + SLOTS

ROW_IDS = 0
ROW_TIDS = ROW_IDS + K_E
ROW_OUT = ROW_TIDS + K_T
ROW_PACK = ROW_OUT + 1
ROWS = 16
GROUP = 16


def grouped(n, size, read, write):
    def one(g, _):
        at = [g * size + u for u in range(size)]
        got = [read(m) for m in at]
        for m, x in zip(at, got):
            write(m, x)
        return 0

    lax.fori_loop(0, n // size, one, 0)


def kernel(
    kappas_h,
    conn_h,
    sends_h,
    owner_h,
    row_h,
    tconn_h,
    diag_e_h,
    faces_h,
    diag_t_h,
    kind_h,
    storage_h,
    rims_h,
    source_h,
    tiles_h,
    warm_h,
    ttiles_h,
    v_out,
    acc,
    kappas,
    sends,
    conn,
    owner,
    row,
    tconn,
    diag_e,
    faces,
    diag_t,
    kind,
    storage,
    rims,
    source,
    tiles,
    warm,
    ttiles,
    tab_v,
    tab,
    ends,
    turn,
    iturn,
    scale,
    diag,
    start0,
    pot,
    field0,
    field1,
    field2,
    field3,
    field4,
    part,
    near,
    wide,
    tnear,
    inc,
    coef,
    flux,
    halo,
    heat,
    outgo,
    income,
    prefix,
    ends_in,
    ends_s,
    local_sem,
    ex_send,
    ex_recv,
    halo_send,
    halo_recv,
    ends_send,
    ends_recv,
    heat_send,
    heat_recv,
):
    e = lax.axis_index("elec")
    t = lax.axis_index("therm")
    field = (field0, field1, field2, field3, field4)
    last = SWEEPS - 1

    def copy_in(src, dst, i):
        return pltpu.make_async_copy(src, dst, local_sem.at[i])

    pairs = (
        (diag_e_h, diag_e),
        (source_h, source),
        (sends_h, sends),
        (conn_h, conn),
        (tconn_h, tconn),
        (owner_h, owner),
        (row_h, row),
        (faces_h, faces),
        (tiles_h, tiles),
        (warm_h, warm),
        (kappas_h, kappas),
        (kind_h, kind),
        (diag_t_h, diag_t),
        (storage_h, storage),
        (rims_h, rims),
        (ttiles_h, ttiles),
    )
    loads = [copy_in(src, dst, i) for i, (src, dst) in enumerate(pairs)]
    for c in loads:
        c.start()

    def partner(bit):
        return e + (1 << bit) - 2 * (1 << bit) * (lax.rem(lax.div(e, 1 << bit), 2))

    barrier = pltpu.get_barrier_semaphore()
    for bit in range(LEVELS):
        pl.semaphore_signal(barrier, inc=1, device_id={"elec": partner(bit)}, device_id_type=MESH)
    for o in range(1, NZ):
        pl.semaphore_signal(
            barrier, inc=1, device_id={"therm": lax.rem(t + o, NZ)}, device_id_type=MESH
        )

    def exchange(k, b):
        return pltpu.make_async_remote_copy(
            src_ref=field[k].at[pl.ds(B + 2 * b, 2)],
            dst_ref=inc.at[k, pl.ds(2 * b, 2)],
            send_sem=ex_send.at[k, b],
            recv_sem=ex_recv.at[k, b],
            device_id={"elec": partner(b)},
            device_id_type=MESH,
        )

    def give(src, dst, send, recv, o):
        return pltpu.make_async_remote_copy(
            src_ref=src,
            dst_ref=dst,
            send_sem=send,
            recv_sem=recv,
            device_id={"therm": lax.rem(t + o, NZ)},
            device_id_type=MESH,
        )

    turn[...] = jnp.zeros_like(turn)
    loads[0].wait()
    turn[0:B, 0:N] = RELAX / diag_e[...]
    turn[B : 2 * B, 0:N] = diag_e[...]
    flipped = turn[...].T[0:N, :]
    loads[1].wait()
    loads[2].wait()
    tiles_of_slots = [sends[s % 2, s // 2] for s in range(SLOTS)]
    spot = lax.broadcasted_iota(jnp.int32, (N, C), 1)

    def column(x, i):
        return jnp.broadcast_to(
            jnp.sum(jnp.where(spot == i, x, 0.0), axis=1, keepdims=True), (N, C)
        )

    for s in range(SLOTS):
        i = tiles_of_slots[s]
        sc = column(flipped, i)
        v = sc * source[i].astype(F32)
        scale[B + s] = sc
        start0[B + s] = v
        pot[B + s] = v
        field0[B + s] = v.astype(BF16)
    pl.semaphore_wait(barrier, LEVELS + NZ - 1)
    for b in reversed(range(LEVELS)):
        exchange(0, b).start()

    def first(g, cur):
        got = []
        for u in range(8):
            i = g * 8 + u
            sc = jnp.broadcast_to(cur[:, u : u + 1], (N, C))
            d = jnp.broadcast_to(cur[:, B + u : B + u + 1], (N, C))
            got.append((i, sc, d, sc * source[i].astype(F32)))
        for i, sc, d, v in got:
            scale[i] = sc
            diag[i] = d
            start0[i] = v
            pot[i] = v
            field0[i] = v.astype(BF16)
        return pltpu.roll(cur, C - 8, 1)

    lax.fori_loop(0, B // 8, first, flipped)
    for s in range(SLOTS):
        diag[B + s] = column(flipped, tiles_of_slots[s] + B)

    def moved(x):
        hit = x
        for s in reversed(range(SLOTS)):
            hit = jnp.where(x == tiles_of_slots[s], B + s, hit)
        return hit

    for i in range(3, 7):
        loads[i].wait()
    tab_v[...] = jnp.zeros_like(tab_v)
    tab_v[ROW_IDS : ROW_IDS + K_E, 0:B] = moved(conn[...])
    tab_v[ROW_TIDS : ROW_TIDS + K_T, 0:B] = tconn[...]
    tab_v[ROW_OUT : ROW_OUT + 1, 0:B] = moved(lax.broadcasted_iota(jnp.int32, (1, B), 1))
    iturn[...] = jnp.zeros_like(iturn)
    iturn[0:1, 0:B] = owner[...]
    iturn[1:2, 0:B] = row[...]
    columns = iturn[...].T
    block = lax.broadcasted_iota(jnp.int32, (B, C), 0)
    lane = lax.broadcasted_iota(jnp.int32, (B, C), 1)
    own_c = jnp.broadcast_to(columns[0:B, 0:1], (B, C))
    row_c = jnp.broadcast_to(columns[0:B, 1:2], (B, C))
    own_r = jnp.broadcast_to(iturn[0:1, :], (B, C))
    row_r = jnp.broadcast_to(iturn[1:2, :], (B, C))
    earlier = (own_r == own_c) & (lane < B) & (row_r * B + lane < row_c * B + block)
    rank = jnp.sum(jnp.where(earlier, 1.0, 0.0), axis=1, keepdims=True).astype(jnp.int32)
    place_c = own_c * CAP + jnp.broadcast_to(rank, (B, C))
    packed = jnp.where(place_c == lane, moved(block), 0)
    tab_v[ROW_PACK : ROW_PACK + 1, :] = jnp.clip(
        jnp.sum(packed, axis=0, keepdims=True), 0, ALL - 1
    )
    c_tab = copy_in(tab_v, tab, 16)
    c_tab.start()

    for z in range(NZ):
        before = jnp.where((own_c == z) & (row_c < lane), 1, 0)
        ends[z, 0:1, :] = jnp.clip(jnp.sum(before, axis=0, keepdims=True), 0, CAP)
        ends[z, 1:8, :] = jnp.zeros((7, C), jnp.int32)
    c_ends = [
        give(ends.at[lax.rem(t + o, NZ)], ends_in.at[o], ends_send.at[o], ends_recv.at[o], o)
        for o in range(1, NZ)
    ]
    for c in c_ends:
        c.start()
    ends_in[0] = ends[t]

    loads[7].wait()
    for s in range(SLOTS):
        for q in range(SLOTS):
            same = (tiles_of_slots[s] == tiles_of_slots[q]).astype(F32)
            wide[s * N : (s + 1) * N, q * N : (q + 1) * N] = (faces[q].astype(F32) * same).astype(BF16)

    loads[8].wait()

    grouped(
        B,
        8,
        lambda i: jnp.concatenate([tiles[i, k] for k in range(K_E)], axis=1),
        lambda i, x: near.__setitem__(i, x),
    )
    c_tab.wait()

    def product(k, i):
        rhs = jnp.concatenate([field[k][tab[ROW_IDS + q, i]] for q in range(K_E)], axis=0)
        return jnp.dot(near[i], rhs, preferred_element_type=F32)

    def sweep(k):
        def update(m, i):
            return pot[m] + start0[m] - RELAX * field[k][m].astype(F32) - scale[m] * product(k, i)

        got = [update(B + s, tiles_of_slots[s]) for s in range(SLOTS)]
        for s in range(SLOTS):
            pot[B + s] = got[s]

        def store(m, new):
            pot[m] = new
            field[k + 1][m] = new.astype(BF16)

        grouped(B, GROUP, lambda m: update(m, m), store)

    EARLY = (SLOTS - 2) * N

    def face_terms(k, then):
        for b in range(LEVELS - 1):
            exchange(k, b).wait_recv()
        part[...] = jnp.dot(
            wide[:, 0:EARLY], inc[k, 0 : SLOTS - 2].reshape(EARLY, C), preferred_element_type=F32
        )
        exchange(k, LEVELS - 1).wait_recv()
        total = part[...] + jnp.dot(
            wide[:, EARLY:], inc[k, SLOTS - 2 :].reshape(2 * N, C), preferred_element_type=F32
        )
        for s in range(SLOTS):
            then(s, total[s * N : (s + 1) * N])

    def finish(k):
        def then(s, g):
            new = pot[B + s] - scale[B + s] * g
            pot[B + s] = new
            field[k + 1][B + s] = new.astype(BF16)

        face_terms(k, then)
        for b in reversed(range(LEVELS)):
            exchange(k + 1, b).start()

    sweep(0)
    finish(0)

    c_up = give(flux.at[pl.ds(B - 2, 2)], halo.at[pl.ds(0, 2)], halo_send.at[0], halo_recv.at[0], 1)
    c_down = give(flux.at[pl.ds(0, 2)], halo.at[pl.ds(2, 2)], halo_send.at[1], halo_recv.at[1], NZ - 1)
    sweep(1)
    for i in range(9, 15):
        loads[i].wait()
    kap = jnp.zeros((B, N), F32)
    for m in range(8):
        kap = kap + jnp.where(kind[...] == m, kappas[m], 0.0)
    turn[0:B, 0:N] = diag_t[...]
    turn[B : 2 * B, 0:N] = kap
    turn[2 * B : 3 * B, 0:N] = STEP / storage[...]
    tflipped = turn[...].T[0:N, :]

    def warmth(g, cur):
        got = []
        for u in range(8):
            i = g * 8 + u
            dt = jnp.broadcast_to(cur[:, u : u + 1], (N, C))
            ka = jnp.broadcast_to(cur[:, B + u : B + u + 1], (N, C))
            co = jnp.broadcast_to(cur[:, 2 * B + u : 2 * B + u + 1], (N, C))
            w = warm[i].astype(F32)
            fl = (ka * (1.0 + 0.4 * jnp.tanh(w)) * w).astype(BF16)
            got.append((i, fl, co, w - co * (dt * fl.astype(F32))))
        for i, fl, co, x in got:
            flux[i] = fl
            coef[i] = co
            acc[i] = x
        return pltpu.roll(cur, C - 8, 1)

    lax.fori_loop(0, B // 8, warmth, tflipped)
    c_up.start()
    c_down.start()
    finish(1)
    sweep(2)
    loads[15].wait()

    grouped(
        B,
        8,
        lambda i: jnp.concatenate([ttiles[i, k] for k in range(K_T)], axis=1),
        lambda i, x: tnear.__setitem__(i, x),
    )
    finish(2)
    sweep(3)

    def conduct(i):
        rhs = jnp.concatenate([flux[tab[ROW_TIDS + q, i]] for q in range(K_T)], axis=0)
        return acc[i] - coef[i] * jnp.dot(tnear[i], rhs, preferred_element_type=F32)

    grouped(B, GROUP, conduct, lambda i, x: acc.__setitem__(i, x))
    finish(3)

    got = [
        diag[B + s] * field4[B + s].astype(F32) + product(last, tiles_of_slots[s])
        for s in range(SLOTS)
    ]
    for s in range(SLOTS):
        pot[B + s] = got[s]

    def natural_heat(m):
        f = field4[m].astype(F32)
        return (f * (diag[m] * f + product(last, m))).astype(BF16)

    grouped(B, GROUP, natural_heat, lambda m, x: heat.__setitem__(m, x))
    grouped(B, 8, lambda i: field4[tab[ROW_OUT, i]], lambda i, x: v_out.__setitem__(i, x))

    c_up.wait()
    c_down.wait()
    for z in range(2):
        low = jnp.dot(rims[z], halo[z], preferred_element_type=F32)
        acc[z] = acc[z] - jnp.where(t > 0, 1.0, 0.0) * coef[z] * low
        high = jnp.dot(rims[2 + z], halo[2 + z], preferred_element_type=F32)
        acc[B - 2 + z] = acc[B - 2 + z] - jnp.where(t < NZ - 1, 1.0, 0.0) * coef[B - 2 + z] * high
    for c in c_ends:
        c.wait()
    c_table = pltpu.make_async_copy(ends_in, ends_s, local_sem.at[17])
    c_table.start()
    c_table.wait()

    def slot_heat(s, g):
        heat[B + s] = (field4[B + s].astype(F32) * (pot[B + s] + g)).astype(BF16)

    face_terms(last, slot_heat)

    order = (1, 7, 2, 6, 3, 5, 4)
    c_heat = {
        o: give(outgo.at[o], income.at[o], heat_send.at[o], heat_recv.at[o], o) for o in order
    }
    for o in order:
        to = lax.rem(t + o, NZ)
        for s in range(CAP):
            outgo[o, s] = heat[tab[ROW_PACK, to * CAP + s]]
        c_heat[o].start()
    for s in range(CAP):
        income[0, s] = heat[tab[ROW_PACK, t * CAP + s]]

    def collect(o):
        run = jnp.zeros((N, C), F32)
        prefix[0] = run
        for s in range(CAP):
            run = run + income[o, s].astype(F32)
            prefix[s + 1] = run

        def row(j):
            upto = prefix[ends_s[o, 0, j + 1]]
            before = prefix[ends_s[o, 0, j]]
            return acc[j] + coef[j] * (upto - before)

        grouped(B, 4, row, lambda j, x: acc.__setitem__(j, x))

    collect(0)
    for o in order:
        c_heat[o].wait_recv()
        collect(o)
    for o in order:
        c_heat[o].wait_send()
    for k in range(SWEEPS):
        for b in range(LEVELS):
            exchange(k, b).wait_send()


def body(
    injected_amperage,
    voltage_self_admittance,
    voltage_coupling_tiles,
    voltage_partner_tile_ids,
    interface_tiles_per_level,
    interface_admittance,
    warmth_receiver_layer,
    warmth_receiver_tile,
    warmth_values,
    warmth_self_coefficient,
    warmth_coupling_tiles,
    warmth_partner_tile_ids,
    layer_boundary_couplings,
    substance_kind,
    reference_material_kappas,
    warmth_storage_per_point,
):
    vmem = pl.BlockSpec(memory_space=pltpu.VMEM)
    hbm = pl.BlockSpec(memory_space=pltpu.HBM)
    dma = pltpu.SemaphoreType.DMA
    V = pltpu.VMEM
    I32 = jnp.int32
    shapes = (
        V((B, N, C), BF16),
        V((B, N, C), F32),
    )
    return pl.pallas_call(
        kernel,
        out_shape=shapes,
        in_specs=[hbm] * 16,
        out_specs=(vmem, vmem),
        scratch_shapes=[
            pltpu.SMEM((8,), F32),
            pltpu.SMEM((2, LEVELS), I32),
            V((K_E, B), I32),
            V((1, B), I32),
            V((1, B), I32),
            V((K_T, B), I32),
            V((B, N), F32),
            V((SLOTS, N, N), BF16),
            V((B, N), F32),
            V((B, N), I32),
            V((B, N), F32),
            V((4, N, N), BF16),
            V((B, N, C), BF16),
            V((B, K_E, N, N), BF16),
            V((B, N, C), BF16),
            V((B, K_T, N, N), BF16),
            V((ROWS, C), I32),
            pltpu.SMEM((ROWS, C), I32),
            V((NZ, 8, C), I32),
            V((C, C), F32),
            V((C, C), I32),
            V((ALL, N, C), F32),
            V((ALL, N, C), F32),
            V((ALL, N, C), F32),
            V((ALL, N, C), F32),
            V((ALL, N, C), BF16),
            V((ALL, N, C), BF16),
            V((ALL, N, C), BF16),
            V((ALL, N, C), BF16),
            V((ALL, N, C), BF16),
            V((SLOTS * N, C), F32),
            V((B, N, K_E * N), BF16),
            V((SLOTS * N, SLOTS * N), BF16),
            V((B, N, K_T * N), BF16),
            V((SWEEPS, SLOTS, N, C), BF16),
            V((B, N, C), F32),
            V((B, N, C), BF16),
            V((4, N, C), BF16),
            V((ALL, N, C), BF16),
            V((NZ, CAP, N, C), BF16),
            V((NZ, CAP, N, C), BF16),
            V((CAP + 1, N, C), F32),
            V((NZ, 8, C), I32),
            pltpu.SMEM((NZ, 8, C), I32),
            dma((20,)),
            dma((SWEEPS, LEVELS)),
            dma((SWEEPS, LEVELS)),
            dma((2,)),
            dma((2,)),
            dma((NZ,)),
            dma((NZ,)),
            dma((NZ,)),
            dma((NZ,)),
        ],
        compiler_params=pltpu.CompilerParams(
            collective_id=0, has_side_effects=True, vmem_limit_bytes=61 * 1024 * 1024
        ),
    )(
        reference_material_kappas,
        voltage_partner_tile_ids.T,
        interface_tiles_per_level.T,
        warmth_receiver_layer.T,
        warmth_receiver_tile.reshape(1, B),
        warmth_partner_tile_ids.T,
        voltage_self_admittance,
        interface_admittance,
        warmth_self_coefficient,
        substance_kind,
        warmth_storage_per_point,
        layer_boundary_couplings,
        injected_amperage,
        voltage_coupling_tiles,
        warmth_values,
        warmth_coupling_tiles,
    )

def solution(mesh):
    both = ("elec", "therm")

    def split(rank):
        return P(both, *([None] * (rank - 1)))

    return jax.shard_map(
        body,
        mesh=mesh,
        in_specs=(
            split(3),
            split(2),
            split(4),
            split(2),
            split(2),
            split(3),
            split(2),
            split(1),
            split(3),
            split(2),
            split(4),
            split(2),
            split(3),
            split(2),
            P(),
            split(2),
        ),
        out_specs=(split(3), split(3)),
        check_vma=False,
    )
```

```python
import functools

import jax
import jax.numpy as jnp
from jax import lax
from jax.experimental import pallas as pl
from jax.experimental.pallas import tpu as pltpu
from jax.sharding import PartitionSpec as P

MESH = pl.DeviceIdType.MESH
F32 = jnp.float32
BF16 = jnp.bfloat16

SWEEPS = 5
RELAX = 0.8
STEP = 0.5
B = 32
N = 64
C = 128
LEVELS = 4
SLOTS = 8
CAP = 8
NZ = 8
K_E = 4
K_T = 3
ALL = B + SLOTS

ROW_IDS = 0
ROW_TIDS = ROW_IDS + K_E
ROW_OUT = ROW_TIDS + K_T
ROW_PACK = ROW_OUT + 1
ROWS = 16
GROUP = 16
FIRST = 7
PIECES = 4


def grouped(n, size, read, write):
    def one(g, _):
        at = [g * size + u for u in range(size)]
        got = [read(m) for m in at]
        for m, x in zip(at, got):
            write(m, x)
        return 0

    lax.fori_loop(0, n // size, one, 0)


def kernel(
    kappas_h,
    conn_h,
    sends_h,
    owner_h,
    row_h,
    tconn_h,
    diag_e_h,
    faces_h,
    diag_t_h,
    kind_h,
    storage_h,
    rims_h,
    source_h,
    tiles_h,
    warm_h,
    ttiles_h,
    v_out,
    acc,
    kappas,
    sends,
    conn,
    owner,
    row,
    tconn,
    diag_e,
    faces,
    diag_t,
    kind,
    storage,
    rims,
    source,
    tiles,
    warm,
    ttiles,
    tab_v,
    tab,
    ends,
    turn,
    iturn,
    scale,
    diag,
    start0,
    pot,
    field0,
    field1,
    field2,
    field3,
    field4,
    part,
    near,
    wide,
    tnear,
    inc,
    coef,
    flux,
    halo,
    heat,
    outgo,
    income,
    prefix,
    ends_in,
    ends_s,
    local_sem,
    ex_send,
    ex_recv,
    halo_send,
    halo_recv,
    ends_send,
    ends_recv,
    heat_send,
    heat_recv,
):
    e = lax.axis_index("elec")
    t = lax.axis_index("therm")
    field = (field0, field1, field2, field3, field4)
    last = SWEEPS - 1

    def copy_in(src, dst, i):
        return pltpu.make_async_copy(src, dst, local_sem.at[i])

    pairs = (
        (diag_e_h, diag_e),
        (source_h, source),
        (sends_h, sends),
        (conn_h, conn),
        (tconn_h, tconn),
        (owner_h, owner),
        (row_h, row),
        (faces_h, faces),
        (tiles_h, tiles),
        (warm_h, warm),
        (kappas_h, kappas),
        (kind_h, kind),
        (diag_t_h, diag_t),
        (storage_h, storage),
        (rims_h, rims),
        (ttiles_h, ttiles),
    )
    loads = [copy_in(src, dst, i) for i, (src, dst) in enumerate(pairs)]
    def partner(bit):
        return e + (1 << bit) - 2 * (1 << bit) * (lax.rem(lax.div(e, 1 << bit), 2))

    barrier = pltpu.get_barrier_semaphore()
    for bit in reversed(range(LEVELS)):
        pl.semaphore_signal(barrier, inc=1, device_id={"elec": partner(bit)}, device_id_type=MESH)
    for o in range(1, NZ):
        pl.semaphore_signal(
            barrier, inc=1, device_id={"therm": lax.rem(t + o, NZ)}, device_id_type=MESH
        )

    def exchange(k, b):
        return pltpu.make_async_remote_copy(
            src_ref=field[k].at[pl.ds(B + 2 * b, 2)],
            dst_ref=inc.at[k, pl.ds(2 * b, 2)],
            send_sem=ex_send.at[k, b],
            recv_sem=ex_recv.at[k, b],
            device_id={"elec": partner(b)},
            device_id_type=MESH,
        )

    def give(src, dst, send, recv, o):
        return pltpu.make_async_remote_copy(
            src_ref=src,
            dst_ref=dst,
            send_sem=send,
            recv_sem=recv,
            device_id={"therm": lax.rem(t + o, NZ)},
            device_id_type=MESH,
        )

    for c in loads[:FIRST]:
        c.start()

    turn[...] = jnp.zeros_like(turn)
    loads[0].wait()
    turn[0:B, 0:N] = RELAX / diag_e[...]
    turn[B : 2 * B, 0:N] = diag_e[...]
    flipped = turn[...].T[0:N, :]
    loads[1].wait()
    for c in loads[FIRST:]:
        c.start()
    loads[2].wait()
    tiles_of_slots = [sends[s % 2, s // 2] for s in range(SLOTS)]
    spot = lax.broadcasted_iota(jnp.int32, (N, C), 1)

    def column(x, i):
        return jnp.broadcast_to(
            jnp.sum(jnp.where(spot == i, x, 0.0), axis=1, keepdims=True), (N, C)
        )

    for s in range(SLOTS):
        i = tiles_of_slots[s]
        sc = column(flipped, i)
        v = sc * source[i].astype(F32)
        scale[B + s] = sc
        start0[B + s] = v
        pot[B + s] = v
        field0[B + s] = v.astype(BF16)
    pl.semaphore_wait(barrier, LEVELS + NZ - 1)
    for b in reversed(range(LEVELS)):
        exchange(0, b).start()

    def first(g, cur):
        got = []
        for u in range(8):
            i = g * 8 + u
            sc = jnp.broadcast_to(cur[:, u : u + 1], (N, C))
            d = jnp.broadcast_to(cur[:, B + u : B + u + 1], (N, C))
            got.append((i, sc, d, sc * source[i].astype(F32)))
        for i, sc, d, v in got:
            scale[i] = sc
            diag[i] = d
            start0[i] = v
            pot[i] = v
            field0[i] = v.astype(BF16)
        return pltpu.roll(cur, C - 8, 1)

    lax.fori_loop(0, B // 8, first, flipped)
    for s in range(SLOTS):
        diag[B + s] = column(flipped, tiles_of_slots[s] + B)

    def moved(x):
        hit = x
        for s in reversed(range(SLOTS)):
            hit = jnp.where(x == tiles_of_slots[s], B + s, hit)
        return hit

    for i in range(3, 7):
        loads[i].wait()
    tab_v[...] = jnp.zeros_like(tab_v)
    tab_v[ROW_IDS : ROW_IDS + K_E, 0:B] = moved(conn[...])
    tab_v[ROW_TIDS : ROW_TIDS + K_T, 0:B] = tconn[...]
    tab_v[ROW_OUT : ROW_OUT + 1, 0:B] = moved(lax.broadcasted_iota(jnp.int32, (1, B), 1))
    iturn[...] = jnp.zeros_like(iturn)
    iturn[0:1, 0:B] = owner[...]
    iturn[1:2, 0:B] = row[...]
    columns = iturn[...].T
    block = lax.broadcasted_iota(jnp.int32, (B, C), 0)
    lane = lax.broadcasted_iota(jnp.int32, (B, C), 1)
    own_c = jnp.broadcast_to(columns[0:B, 0:1], (B, C))
    row_c = jnp.broadcast_to(columns[0:B, 1:2], (B, C))
    own_r = jnp.broadcast_to(iturn[0:1, :], (B, C))
    row_r = jnp.broadcast_to(iturn[1:2, :], (B, C))
    earlier = (own_r == own_c) & (lane < B) & (row_r * B + lane < row_c * B + block)
    rank = jnp.sum(jnp.where(earlier, 1.0, 0.0), axis=1, keepdims=True).astype(jnp.int32)
    place_c = own_c * CAP + jnp.broadcast_to(rank, (B, C))
    packed = jnp.where(place_c == lane, moved(block), 0)
    tab_v[ROW_PACK : ROW_PACK + 1, :] = jnp.clip(
        jnp.sum(packed, axis=0, keepdims=True), 0, ALL - 1
    )
    c_tab = copy_in(tab_v, tab, 16)
    c_tab.start()

    for z in range(NZ):
        before = jnp.where((own_c == z) & (row_c < lane), 1, 0)
        ends[z, 0:1, :] = jnp.clip(jnp.sum(before, axis=0, keepdims=True), 0, CAP)
        ends[z, 1:8, :] = jnp.zeros((7, C), jnp.int32)
    c_ends = [
        give(ends.at[lax.rem(t + o, NZ)], ends_in.at[o], ends_send.at[o], ends_recv.at[o], o)
        for o in range(1, NZ)
    ]
    for c in c_ends:
        c.start()
    ends_in[0] = ends[t]

    loads[7].wait()
    for s in range(SLOTS):
        for q in range(SLOTS):
            same = (tiles_of_slots[s] == tiles_of_slots[q]).astype(F32)
            wide[s * N : (s + 1) * N, q * N : (q + 1) * N] = (faces[q].astype(F32) * same).astype(BF16)

    loads[8].wait()

    grouped(
        B,
        8,
        lambda i: jnp.concatenate([tiles[i, k] for k in range(K_E)], axis=1),
        lambda i, x: near.__setitem__(i, x),
    )
    c_tab.wait()

    def product(k, i):
        rhs = jnp.concatenate([field[k][tab[ROW_IDS + q, i]] for q in range(K_E)], axis=0)
        return jnp.dot(near[i], rhs, preferred_element_type=F32)

    def sweep(k):
        def update(m, i):
            return pot[m] + start0[m] - RELAX * field[k][m].astype(F32) - scale[m] * product(k, i)

        got = [update(B + s, tiles_of_slots[s]) for s in range(SLOTS)]
        for s in range(SLOTS):
            pot[B + s] = got[s]

        def store(m, new):
            pot[m] = new
            field[k + 1][m] = new.astype(BF16)

        grouped(B, GROUP, lambda m: update(m, m), store)

    EARLY = (SLOTS - 2) * N

    def face_update(k, low, factor):
        for b in range(LEVELS - 1):
            exchange(k, b).wait_recv()
        some = jnp.dot(
            wide[:, 0:EARLY], inc[k, 0 : SLOTS - 2].reshape(EARLY, C), preferred_element_type=F32
        )
        for s in range(SLOTS):
            rows = slice(s * N, (s + 1) * N)
            part[rows] = low(s) + factor(s) * some[rows]
        exchange(k, LEVELS - 1).wait_recv()
        more = jnp.dot(
            wide[:, EARLY:], inc[k, SLOTS - 2 :].reshape(2 * N, C), preferred_element_type=F32
        )
        rows = [slice(s * N, (s + 1) * N) for s in range(SLOTS)]
        return [part[rows[s]] + factor(s) * more[rows[s]] for s in range(SLOTS)]

    def finish(k):
        new = face_update(k, lambda s: pot[B + s], lambda s: -scale[B + s])
        for s in range(SLOTS):
            field[k + 1][B + s] = new[s].astype(BF16)
        for b in reversed(range(LEVELS)):
            exchange(k + 1, b).start()
        for s in range(SLOTS):
            pot[B + s] = new[s]

    sweep(0)
    finish(0)

    c_up = give(flux.at[pl.ds(B - 2, 2)], halo.at[pl.ds(0, 2)], halo_send.at[0], halo_recv.at[0], 1)
    c_down = give(flux.at[pl.ds(0, 2)], halo.at[pl.ds(2, 2)], halo_send.at[1], halo_recv.at[1], NZ - 1)
    sweep(1)
    for i in range(9, 15):
        loads[i].wait()
    kap = jnp.zeros((B, N), F32)
    for m in range(8):
        kap = kap + jnp.where(kind[...] == m, kappas[m], 0.0)
    turn[0:B, 0:N] = diag_t[...]
    turn[B : 2 * B, 0:N] = kap
    turn[2 * B : 3 * B, 0:N] = STEP / storage[...]
    tflipped = turn[...].T[0:N, :]

    def warmth(g, cur):
        got = []
        for u in range(8):
            i = g * 8 + u
            dt = jnp.broadcast_to(cur[:, u : u + 1], (N, C))
            ka = jnp.broadcast_to(cur[:, B + u : B + u + 1], (N, C))
            co = jnp.broadcast_to(cur[:, 2 * B + u : 2 * B + u + 1], (N, C))
            w = warm[i].astype(F32)
            fl = (ka * (1.0 + 0.4 * jnp.tanh(w)) * w).astype(BF16)
            got.append((i, fl, co, w - co * (dt * fl.astype(F32))))
        for i, fl, co, x in got:
            flux[i] = fl
            coef[i] = co
            acc[i] = x
        return pltpu.roll(cur, C - 8, 1)

    lax.fori_loop(0, B // 8, warmth, tflipped)
    c_up.start()
    c_down.start()
    finish(1)
    sweep(2)
    loads[15].wait()

    grouped(
        B,
        8,
        lambda i: jnp.concatenate([ttiles[i, k] for k in range(K_T)], axis=1),
        lambda i, x: tnear.__setitem__(i, x),
    )
    finish(2)
    sweep(3)

    def conduct(i):
        rhs = jnp.concatenate([flux[tab[ROW_TIDS + q, i]] for q in range(K_T)], axis=0)
        return acc[i] - coef[i] * jnp.dot(tnear[i], rhs, preferred_element_type=F32)

    grouped(B, GROUP, conduct, lambda i, x: acc.__setitem__(i, x))
    finish(3)

    got = [
        diag[B + s] * field4[B + s].astype(F32) + product(last, tiles_of_slots[s])
        for s in range(SLOTS)
    ]
    for s in range(SLOTS):
        pot[B + s] = got[s]

    def natural_heat(m):
        f = field4[m].astype(F32)
        return (f * (diag[m] * f + product(last, m))).astype(BF16)

    grouped(B, GROUP, natural_heat, lambda m, x: heat.__setitem__(m, x))
    grouped(B, 8, lambda i: field4[tab[ROW_OUT, i]], lambda i, x: v_out.__setitem__(i, x))

    c_up.wait()
    c_down.wait()
    for z in range(2):
        low = jnp.dot(rims[z], halo[z], preferred_element_type=F32)
        acc[z] = acc[z] - jnp.where(t > 0, 1.0, 0.0) * coef[z] * low
        high = jnp.dot(rims[2 + z], halo[2 + z], preferred_element_type=F32)
        acc[B - 2 + z] = acc[B - 2 + z] - jnp.where(t < NZ - 1, 1.0, 0.0) * coef[B - 2 + z] * high
    for c in c_ends:
        c.wait()
    c_table = pltpu.make_async_copy(ends_in, ends_s, local_sem.at[17])
    c_table.start()
    c_table.wait()

    current = face_update(last, lambda s: pot[B + s], lambda s: 1.0)
    for s in range(SLOTS):
        heat[B + s] = (field4[B + s].astype(F32) * current[s]).astype(BF16)

    order = (1, 7, 2, 6, 3, 5, 4)
    c_heat = {
        o: give(outgo.at[o], income.at[o], heat_send.at[o], heat_recv.at[o], o) for o in order
    }
    for o in order:
        to = lax.rem(t + o, NZ)
        for s in range(CAP):
            outgo[o, s] = heat[tab[ROW_PACK, to * CAP + s]]
        c_heat[o].start()
    for s in range(CAP):
        income[0, s] = heat[tab[ROW_PACK, t * CAP + s]]

    def collect(o):
        run = jnp.zeros((N, C), F32)
        prefix[0] = run
        for s in range(CAP):
            run = run + income[o, s].astype(F32)
            prefix[s + 1] = run

        def row(j):
            upto = prefix[ends_s[o, 0, j + 1]]
            before = prefix[ends_s[o, 0, j]]
            return acc[j] + coef[j] * (upto - before)

        grouped(B, 4, row, lambda j, x: acc.__setitem__(j, x))

    collect(0)
    for o in order:
        c_heat[o].wait_recv()
        collect(o)
    for o in order:
        c_heat[o].wait_send()
    for k in range(SWEEPS):
        for b in range(LEVELS):
            exchange(k, b).wait_send()


def hand_over(v, w, v_out, w_out, sems):
    size = B // PIECES
    copies = []
    for i in range(PIECES):
        piece = pl.ds(i * size, size)
        copies.append(pltpu.make_async_copy(w.at[piece], w_out.at[piece], sems.at[0, i]))
        copies.append(pltpu.make_async_copy(v.at[piece], v_out.at[piece], sems.at[1, i]))
    for c in copies:
        c.start()
    for c in copies:
        c.wait()


def body(
    injected_amperage,
    voltage_self_admittance,
    voltage_coupling_tiles,
    voltage_partner_tile_ids,
    interface_tiles_per_level,
    interface_admittance,
    warmth_receiver_layer,
    warmth_receiver_tile,
    warmth_values,
    warmth_self_coefficient,
    warmth_coupling_tiles,
    warmth_partner_tile_ids,
    layer_boundary_couplings,
    substance_kind,
    reference_material_kappas,
    warmth_storage_per_point,
):
    vmem = pl.BlockSpec(memory_space=pltpu.VMEM)
    hbm = pl.BlockSpec(memory_space=pltpu.HBM)
    dma = pltpu.SemaphoreType.DMA
    V = pltpu.VMEM
    I32 = jnp.int32
    shapes = (
        V((B, N, C), BF16),
        V((B, N, C), F32),
    )
    v, w = pl.pallas_call(
        kernel,
        out_shape=shapes,
        in_specs=[hbm] * 16,
        out_specs=(vmem, vmem),
        scratch_shapes=[
            pltpu.SMEM((8,), F32),
            pltpu.SMEM((2, LEVELS), I32),
            V((K_E, B), I32),
            V((1, B), I32),
            V((1, B), I32),
            V((K_T, B), I32),
            V((B, N), F32),
            V((SLOTS, N, N), BF16),
            V((B, N), F32),
            V((B, N), I32),
            V((B, N), F32),
            V((4, N, N), BF16),
            V((B, N, C), BF16),
            V((B, K_E, N, N), BF16),
            V((B, N, C), BF16),
            V((B, K_T, N, N), BF16),
            V((ROWS, C), I32),
            pltpu.SMEM((ROWS, C), I32),
            V((NZ, 8, C), I32),
            V((C, C), F32),
            V((C, C), I32),
            V((ALL, N, C), F32),
            V((ALL, N, C), F32),
            V((ALL, N, C), F32),
            V((ALL, N, C), F32),
            V((ALL, N, C), BF16),
            V((ALL, N, C), BF16),
            V((ALL, N, C), BF16),
            V((ALL, N, C), BF16),
            V((ALL, N, C), BF16),
            V((SLOTS * N, C), F32),
            V((B, N, K_E * N), BF16),
            V((SLOTS * N, SLOTS * N), BF16),
            V((B, N, K_T * N), BF16),
            V((SWEEPS, SLOTS, N, C), BF16),
            V((B, N, C), F32),
            V((B, N, C), BF16),
            V((4, N, C), BF16),
            V((ALL, N, C), BF16),
            V((NZ, CAP, N, C), BF16),
            V((NZ, CAP, N, C), BF16),
            V((CAP + 1, N, C), F32),
            V((NZ, 8, C), I32),
            pltpu.SMEM((NZ, 8, C), I32),
            dma((20,)),
            dma((SWEEPS, LEVELS)),
            dma((SWEEPS, LEVELS)),
            dma((2,)),
            dma((2,)),
            dma((NZ,)),
            dma((NZ,)),
            dma((NZ,)),
            dma((NZ,)),
        ],
        compiler_params=pltpu.CompilerParams(
            collective_id=0, has_side_effects=True, vmem_limit_bytes=61 * 1024 * 1024
        ),
    )(
        reference_material_kappas,
        voltage_partner_tile_ids.T,
        interface_tiles_per_level.T,
        warmth_receiver_layer.T,
        warmth_receiver_tile.reshape(1, B),
        warmth_partner_tile_ids.T,
        voltage_self_admittance,
        interface_admittance,
        warmth_self_coefficient,
        substance_kind,
        warmth_storage_per_point,
        layer_boundary_couplings,
        injected_amperage,
        voltage_coupling_tiles,
        warmth_values,
        warmth_coupling_tiles,
    )
    return pl.pallas_call(
        hand_over,
        out_shape=(
            jax.ShapeDtypeStruct((B, N, C), BF16),
            jax.ShapeDtypeStruct((B, N, C), F32),
        ),
        in_specs=[vmem, vmem],
        out_specs=(hbm, hbm),
        scratch_shapes=[dma((2, PIECES))],
    )(
        pltpu.with_memory_space_constraint(v, pltpu.VMEM),
        pltpu.with_memory_space_constraint(w, pltpu.VMEM),
    )

def solution(mesh):
    both = ("elec", "therm")

    def split(rank):
        return P(both, *([None] * (rank - 1)))

    return jax.shard_map(
        body,
        mesh=mesh,
        in_specs=(
            split(3),
            split(2),
            split(4),
            split(2),
            split(2),
            split(3),
            split(2),
            split(1),
            split(3),
            split(2),
            split(4),
            split(2),
            split(3),
            split(2),
            P(),
            split(2),
        ),
        out_specs=(split(3), split(3)),
        check_vma=False,
    )
```

```python
import functools

import jax
import jax.numpy as jnp
from jax import lax
from jax.experimental import pallas as pl
from jax.experimental.pallas import tpu as pltpu
from jax.sharding import PartitionSpec as P

MESH = pl.DeviceIdType.MESH
F32 = jnp.float32
BF16 = jnp.bfloat16

SWEEPS = 5
RELAX = 0.8
STEP = 0.5
B = 32
N = 64
C = 128
LEVELS = 4
SLOTS = 8
CAP = 8
NZ = 8
K_E = 4
K_T = 3
ALL = B + SLOTS

ROW_IDS = 0
ROW_TIDS = ROW_IDS + K_E
ROW_OUT = ROW_TIDS + K_T
ROW_PACK = ROW_OUT + 1
ROWS = 16
GROUP = 8
FIRST = 3
PIECES = 4


def grouped(n, size, read, write):
    def one(g, _):
        at = [g * size + u for u in range(size)]
        got = [read(m) for m in at]
        for m, x in zip(at, got):
            write(m, x)
        return 0

    lax.fori_loop(0, n // size, one, 0)


def kernel(
    kappas_h,
    conn_h,
    sends_h,
    owner_h,
    row_h,
    tconn_h,
    diag_e_h,
    faces_h,
    diag_t_h,
    kind_h,
    storage_h,
    rims_h,
    source_h,
    tiles_h,
    warm_h,
    ttiles_h,
    v_out,
    acc,
    kappas,
    sends,
    conn,
    owner,
    row,
    tconn,
    diag_e,
    faces,
    diag_t,
    kind,
    storage,
    rims,
    source,
    tiles,
    warm,
    ttiles,
    tab_v,
    tab,
    ends,
    turn,
    iturn,
    scale,
    diag,
    start0,
    pot,
    field0,
    field1,
    field2,
    field3,
    field4,
    part,
    near,
    wide,
    tnear,
    inc,
    coef,
    flux,
    halo,
    heat,
    outgo,
    income,
    prefix,
    ends_in,
    ends_s,
    local_sem,
    ex_send,
    ex_recv,
    halo_send,
    halo_recv,
    ends_send,
    ends_recv,
    heat_send,
    heat_recv,
):
    e = lax.axis_index("elec")
    t = lax.axis_index("therm")
    field = (field0, field1, field2, field3, field4)
    last = SWEEPS - 1

    def copy_in(src, dst, i):
        return pltpu.make_async_copy(src, dst, local_sem.at[i])

    pairs = (
        (diag_e_h, diag_e),
        (source_h, source),
        (sends_h, sends),
        (conn_h, conn),
        (tconn_h, tconn),
        (owner_h, owner),
        (row_h, row),
        (faces_h, faces),
        (tiles_h, tiles),
        (warm_h, warm),
        (kappas_h, kappas),
        (kind_h, kind),
        (diag_t_h, diag_t),
        (storage_h, storage),
        (rims_h, rims),
        (ttiles_h, ttiles),
    )
    loads = [copy_in(src, dst, i) for i, (src, dst) in enumerate(pairs)]
    def partner(bit):
        return e + (1 << bit) - 2 * (1 << bit) * (lax.rem(lax.div(e, 1 << bit), 2))

    barrier = pltpu.get_barrier_semaphore()
    for bit in reversed(range(LEVELS)):
        pl.semaphore_signal(barrier, inc=1, device_id={"elec": partner(bit)}, device_id_type=MESH)
    for o in range(1, NZ):
        pl.semaphore_signal(
            barrier, inc=1, device_id={"therm": lax.rem(t + o, NZ)}, device_id_type=MESH
        )

    def exchange(k, b):
        return pltpu.make_async_remote_copy(
            src_ref=field[k].at[pl.ds(B + 2 * b, 2)],
            dst_ref=inc.at[k, pl.ds(2 * b, 2)],
            send_sem=ex_send.at[k, b],
            recv_sem=ex_recv.at[k, b],
            device_id={"elec": partner(b)},
            device_id_type=MESH,
        )

    def give(src, dst, send, recv, o):
        return pltpu.make_async_remote_copy(
            src_ref=src,
            dst_ref=dst,
            send_sem=send,
            recv_sem=recv,
            device_id={"therm": lax.rem(t + o, NZ)},
            device_id_type=MESH,
        )

    for c in loads[:FIRST]:
        c.start()

    turn[...] = jnp.zeros_like(turn)
    loads[0].wait()
    turn[0:B, 0:N] = RELAX / diag_e[...]
    turn[B : 2 * B, 0:N] = diag_e[...]
    flipped = turn[...].T[0:N, :]
    loads[1].wait()
    for c in loads[FIRST:]:
        c.start()
    loads[2].wait()
    tiles_of_slots = [sends[s % 2, s // 2] for s in range(SLOTS)]
    spot = lax.broadcasted_iota(jnp.int32, (N, C), 1)

    def column(x, i):
        return jnp.broadcast_to(
            jnp.sum(jnp.where(spot == i, x, 0.0), axis=1, keepdims=True), (N, C)
        )

    for s in range(SLOTS):
        i = tiles_of_slots[s]
        sc = column(flipped, i)
        v = sc * source[i].astype(F32)
        scale[B + s] = sc
        start0[B + s] = v
        pot[B + s] = v
        field0[B + s] = v.astype(BF16)
    pl.semaphore_wait(barrier, LEVELS + NZ - 1)
    for b in reversed(range(LEVELS)):
        exchange(0, b).start()

    def first(g, cur):
        got = []
        for u in range(8):
            i = g * 8 + u
            sc = jnp.broadcast_to(cur[:, u : u + 1], (N, C))
            d = jnp.broadcast_to(cur[:, B + u : B + u + 1], (N, C))
            got.append((i, sc, d, sc * source[i].astype(F32)))
        for i, sc, d, v in got:
            scale[i] = sc
            diag[i] = d
            start0[i] = v
            pot[i] = v
            field0[i] = v.astype(BF16)
        return pltpu.roll(cur, C - 8, 1)

    lax.fori_loop(0, B // 8, first, flipped)
    for s in range(SLOTS):
        diag[B + s] = column(flipped, tiles_of_slots[s] + B)

    def moved(x):
        hit = x
        for s in reversed(range(SLOTS)):
            hit = jnp.where(x == tiles_of_slots[s], B + s, hit)
        return hit

    for i in range(3, 7):
        loads[i].wait()
    tab_v[...] = jnp.zeros_like(tab_v)
    tab_v[ROW_IDS : ROW_IDS + K_E, 0:B] = moved(conn[...])
    tab_v[ROW_TIDS : ROW_TIDS + K_T, 0:B] = tconn[...]
    tab_v[ROW_OUT : ROW_OUT + 1, 0:B] = moved(lax.broadcasted_iota(jnp.int32, (1, B), 1))
    iturn[...] = jnp.zeros_like(iturn)
    iturn[0:1, 0:B] = owner[...]
    iturn[1:2, 0:B] = row[...]
    columns = iturn[...].T
    block = lax.broadcasted_iota(jnp.int32, (B, C), 0)
    lane = lax.broadcasted_iota(jnp.int32, (B, C), 1)
    own_c = jnp.broadcast_to(columns[0:B, 0:1], (B, C))
    row_c = jnp.broadcast_to(columns[0:B, 1:2], (B, C))
    own_r = jnp.broadcast_to(iturn[0:1, :], (B, C))
    row_r = jnp.broadcast_to(iturn[1:2, :], (B, C))
    earlier = (own_r == own_c) & (lane < B) & (row_r * B + lane < row_c * B + block)
    rank = jnp.sum(jnp.where(earlier, 1.0, 0.0), axis=1, keepdims=True).astype(jnp.int32)
    place_c = own_c * CAP + jnp.broadcast_to(rank, (B, C))
    packed = jnp.where(place_c == lane, moved(block), 0)
    tab_v[ROW_PACK : ROW_PACK + 1, :] = jnp.clip(
        jnp.sum(packed, axis=0, keepdims=True), 0, ALL - 1
    )
    c_tab = copy_in(tab_v, tab, 16)
    c_tab.start()

    for z in range(NZ):
        before = jnp.where((own_c == z) & (row_c < lane), 1, 0)
        ends[z, 0:1, :] = jnp.clip(jnp.sum(before, axis=0, keepdims=True), 0, CAP)
        ends[z, 1:8, :] = jnp.zeros((7, C), jnp.int32)
    c_ends = [
        give(ends.at[lax.rem(t + o, NZ)], ends_in.at[o], ends_send.at[o], ends_recv.at[o], o)
        for o in range(1, NZ)
    ]
    for c in c_ends:
        c.start()
    ends_in[0] = ends[t]

    loads[7].wait()
    for s in range(SLOTS):
        for q in range(SLOTS):
            same = (tiles_of_slots[s] == tiles_of_slots[q]).astype(F32)
            wide[s * N : (s + 1) * N, q * N : (q + 1) * N] = (faces[q].astype(F32) * same).astype(BF16)

    loads[8].wait()

    grouped(
        B,
        8,
        lambda i: jnp.concatenate([tiles[i, k] for k in range(K_E)], axis=1),
        lambda i, x: near.__setitem__(i, x),
    )
    c_tab.wait()

    def product(k, i):
        rhs = jnp.concatenate([field[k][tab[ROW_IDS + q, i]] for q in range(K_E)], axis=0)
        return jnp.dot(near[i], rhs, preferred_element_type=F32)

    def sweep(k):
        def update(m, i):
            return pot[m] + start0[m] - RELAX * field[k][m].astype(F32) - scale[m] * product(k, i)

        got = [update(B + s, tiles_of_slots[s]) for s in range(SLOTS)]
        for s in range(SLOTS):
            pot[B + s] = got[s]

        def store(m, new):
            pot[m] = new
            field[k + 1][m] = new.astype(BF16)

        grouped(B, GROUP, lambda m: update(m, m), store)

    EARLY = (SLOTS - 2) * N

    def face_update(k, low, factor):
        for b in range(LEVELS - 1):
            exchange(k, b).wait_recv()
        some = jnp.dot(
            wide[:, 0:EARLY], inc[k, 0 : SLOTS - 2].reshape(EARLY, C), preferred_element_type=F32
        )
        for s in range(SLOTS):
            rows = slice(s * N, (s + 1) * N)
            part[rows] = low(s) + factor(s) * some[rows]
        exchange(k, LEVELS - 1).wait_recv()
        more = jnp.dot(
            wide[:, EARLY:], inc[k, SLOTS - 2 :].reshape(2 * N, C), preferred_element_type=F32
        )
        rows = [slice(s * N, (s + 1) * N) for s in range(SLOTS)]
        return [part[rows[s]] + factor(s) * more[rows[s]] for s in range(SLOTS)]

    def finish(k):
        new = face_update(k, lambda s: pot[B + s], lambda s: -scale[B + s])
        for s in range(SLOTS):
            field[k + 1][B + s] = new[s].astype(BF16)
        for b in reversed(range(LEVELS)):
            exchange(k + 1, b).start()
        for s in range(SLOTS):
            pot[B + s] = new[s]

    sweep(0)
    finish(0)

    c_up = give(flux.at[pl.ds(B - 2, 2)], halo.at[pl.ds(0, 2)], halo_send.at[0], halo_recv.at[0], 1)
    c_down = give(flux.at[pl.ds(0, 2)], halo.at[pl.ds(2, 2)], halo_send.at[1], halo_recv.at[1], NZ - 1)
    sweep(1)
    for i in range(9, 15):
        loads[i].wait()
    kap = jnp.zeros((B, N), F32)
    for m in range(8):
        kap = kap + jnp.where(kind[...] == m, kappas[m], 0.0)
    turn[0:B, 0:N] = diag_t[...]
    turn[B : 2 * B, 0:N] = kap
    turn[2 * B : 3 * B, 0:N] = STEP / storage[...]
    tflipped = turn[...].T[0:N, :]

    def warmth(g, cur):
        got = []
        for u in range(8):
            i = g * 8 + u
            dt = jnp.broadcast_to(cur[:, u : u + 1], (N, C))
            ka = jnp.broadcast_to(cur[:, B + u : B + u + 1], (N, C))
            co = jnp.broadcast_to(cur[:, 2 * B + u : 2 * B + u + 1], (N, C))
            w = warm[i].astype(F32)
            fl = (ka * (1.0 + 0.4 * jnp.tanh(w)) * w).astype(BF16)
            got.append((i, fl, co, w - co * (dt * fl.astype(F32))))
        for i, fl, co, x in got:
            flux[i] = fl
            coef[i] = co
            acc[i] = x
        return pltpu.roll(cur, C - 8, 1)

    lax.fori_loop(0, B // 8, warmth, tflipped)
    c_up.start()
    c_down.start()
    finish(1)
    sweep(2)
    loads[15].wait()

    grouped(
        B,
        8,
        lambda i: jnp.concatenate([ttiles[i, k] for k in range(K_T)], axis=1),
        lambda i, x: tnear.__setitem__(i, x),
    )
    finish(2)
    sweep(3)

    def conduct(i):
        rhs = jnp.concatenate([flux[tab[ROW_TIDS + q, i]] for q in range(K_T)], axis=0)
        return acc[i] - coef[i] * jnp.dot(tnear[i], rhs, preferred_element_type=F32)

    grouped(B, GROUP, conduct, lambda i, x: acc.__setitem__(i, x))
    finish(3)

    got = [
        diag[B + s] * field4[B + s].astype(F32) + product(last, tiles_of_slots[s])
        for s in range(SLOTS)
    ]
    for s in range(SLOTS):
        pot[B + s] = got[s]

    def natural_heat(m):
        f = field4[m].astype(F32)
        return (f * (diag[m] * f + product(last, m))).astype(BF16)

    grouped(B, GROUP, natural_heat, lambda m, x: heat.__setitem__(m, x))
    grouped(B, 8, lambda i: field4[tab[ROW_OUT, i]], lambda i, x: v_out.__setitem__(i, x))

    c_up.wait()
    c_down.wait()
    for z in range(2):
        low = jnp.dot(rims[z], halo[z], preferred_element_type=F32)
        acc[z] = acc[z] - jnp.where(t > 0, 1.0, 0.0) * coef[z] * low
        high = jnp.dot(rims[2 + z], halo[2 + z], preferred_element_type=F32)
        acc[B - 2 + z] = acc[B - 2 + z] - jnp.where(t < NZ - 1, 1.0, 0.0) * coef[B - 2 + z] * high
    for c in c_ends:
        c.wait()
    c_table = pltpu.make_async_copy(ends_in, ends_s, local_sem.at[17])
    c_table.start()
    c_table.wait()

    current = face_update(last, lambda s: pot[B + s], lambda s: 1.0)
    for s in range(SLOTS):
        heat[B + s] = (field4[B + s].astype(F32) * current[s]).astype(BF16)

    core = lax.rem(e, 2)
    order = [
        jnp.where(core == 0, x, y) for x, y in zip((1, 7, 2, 6, 3, 5, 4), (4, 3, 5, 2, 6, 1, 7))
    ]
    c_heat = [
        give(outgo.at[o], income.at[o], heat_send.at[o], heat_recv.at[o], o) for o in order
    ]
    for o, c in zip(order, c_heat):
        to = lax.rem(t + o, NZ)
        for s in range(CAP):
            outgo[o, s] = heat[tab[ROW_PACK, to * CAP + s]]
        c.start()
    for s in range(CAP):
        income[0, s] = heat[tab[ROW_PACK, t * CAP + s]]

    def collect(o):
        run = jnp.zeros((N, C), F32)
        prefix[0] = run
        for s in range(CAP):
            run = run + income[o, s].astype(F32)
            prefix[s + 1] = run

        def row(j):
            upto = prefix[ends_s[o, 0, j + 1]]
            before = prefix[ends_s[o, 0, j]]
            return acc[j] + coef[j] * (upto - before)

        grouped(B, 4, row, lambda j, x: acc.__setitem__(j, x))

    collect(0)
    for o, c in zip(order, c_heat):
        c.wait_recv()
        collect(o)
    for c in c_heat:
        c.wait_send()
    for k in range(SWEEPS):
        for b in range(LEVELS):
            exchange(k, b).wait_send()


def hand_over(v, w, v_out, w_out, sems):
    size = B // PIECES
    copies = []
    for i in range(PIECES):
        piece = pl.ds(i * size, size)
        copies.append(pltpu.make_async_copy(w.at[piece], w_out.at[piece], sems.at[0, i]))
        copies.append(pltpu.make_async_copy(v.at[piece], v_out.at[piece], sems.at[1, i]))
    for c in copies:
        c.start()
    for c in copies:
        c.wait()


def body(
    injected_amperage,
    voltage_self_admittance,
    voltage_coupling_tiles,
    voltage_partner_tile_ids,
    interface_tiles_per_level,
    interface_admittance,
    warmth_receiver_layer,
    warmth_receiver_tile,
    warmth_values,
    warmth_self_coefficient,
    warmth_coupling_tiles,
    warmth_partner_tile_ids,
    layer_boundary_couplings,
    substance_kind,
    reference_material_kappas,
    warmth_storage_per_point,
):
    vmem = pl.BlockSpec(memory_space=pltpu.VMEM)
    hbm = pl.BlockSpec(memory_space=pltpu.HBM)
    dma = pltpu.SemaphoreType.DMA
    V = pltpu.VMEM
    I32 = jnp.int32
    shapes = (
        V((B, N, C), BF16),
        V((B, N, C), F32),
    )
    v, w = pl.pallas_call(
        kernel,
        out_shape=shapes,
        in_specs=[hbm] * 16,
        out_specs=(vmem, vmem),
        scratch_shapes=[
            pltpu.SMEM((8,), F32),
            pltpu.SMEM((2, LEVELS), I32),
            V((K_E, B), I32),
            V((1, B), I32),
            V((1, B), I32),
            V((K_T, B), I32),
            V((B, N), F32),
            V((SLOTS, N, N), BF16),
            V((B, N), F32),
            V((B, N), I32),
            V((B, N), F32),
            V((4, N, N), BF16),
            V((B, N, C), BF16),
            V((B, K_E, N, N), BF16),
            V((B, N, C), BF16),
            V((B, K_T, N, N), BF16),
            V((ROWS, C), I32),
            pltpu.SMEM((ROWS, C), I32),
            V((NZ, 8, C), I32),
            V((C, C), F32),
            V((C, C), I32),
            V((ALL, N, C), F32),
            V((ALL, N, C), F32),
            V((ALL, N, C), F32),
            V((ALL, N, C), F32),
            V((ALL, N, C), BF16),
            V((ALL, N, C), BF16),
            V((ALL, N, C), BF16),
            V((ALL, N, C), BF16),
            V((ALL, N, C), BF16),
            V((SLOTS * N, C), F32),
            V((B, N, K_E * N), BF16),
            V((SLOTS * N, SLOTS * N), BF16),
            V((B, N, K_T * N), BF16),
            V((SWEEPS, SLOTS, N, C), BF16),
            V((B, N, C), F32),
            V((B, N, C), BF16),
            V((4, N, C), BF16),
            V((ALL, N, C), BF16),
            V((NZ, CAP, N, C), BF16),
            V((NZ, CAP, N, C), BF16),
            V((CAP + 1, N, C), F32),
            V((NZ, 8, C), I32),
            pltpu.SMEM((NZ, 8, C), I32),
            dma((20,)),
            dma((SWEEPS, LEVELS)),
            dma((SWEEPS, LEVELS)),
            dma((2,)),
            dma((2,)),
            dma((NZ,)),
            dma((NZ,)),
            dma((NZ,)),
            dma((NZ,)),
        ],
        compiler_params=pltpu.CompilerParams(
            collective_id=0, has_side_effects=True, vmem_limit_bytes=61 * 1024 * 1024
        ),
    )(
        reference_material_kappas,
        voltage_partner_tile_ids.T,
        interface_tiles_per_level.T,
        warmth_receiver_layer.T,
        warmth_receiver_tile.reshape(1, B),
        warmth_partner_tile_ids.T,
        voltage_self_admittance,
        interface_admittance,
        warmth_self_coefficient,
        substance_kind,
        warmth_storage_per_point,
        layer_boundary_couplings,
        injected_amperage,
        voltage_coupling_tiles,
        warmth_values,
        warmth_coupling_tiles,
    )
    return pl.pallas_call(
        hand_over,
        out_shape=(
            jax.ShapeDtypeStruct((B, N, C), BF16),
            jax.ShapeDtypeStruct((B, N, C), F32),
        ),
        in_specs=[vmem, vmem],
        out_specs=(hbm, hbm),
        scratch_shapes=[dma((2, PIECES))],
    )(
        pltpu.with_memory_space_constraint(v, pltpu.VMEM),
        pltpu.with_memory_space_constraint(w, pltpu.VMEM),
    )

def solution(mesh):
    both = ("elec", "therm")

    def split(rank):
        return P(both, *([None] * (rank - 1)))

    return jax.shard_map(
        body,
        mesh=mesh,
        in_specs=(
            split(3),
            split(2),
            split(4),
            split(2),
            split(2),
            split(3),
            split(2),
            split(1),
            split(3),
            split(2),
            split(4),
            split(2),
            split(3),
            split(2),
            P(),
            split(2),
        ),
        out_specs=(split(3), split(3)),
        check_vma=False,
    )
```
